256 devices in a mesh: dp: 16 (over z, y_hi), tensor: 16 (over x, y_lo, core).
Axes of the slice: x: 4, y: 4 (y_hi: 2, y_lo: 2; y = y_hi * 2 + y_lo), z: 8, core: 2. Of those that a mesh axis runs over, the one named last changes fastest.
Arguments:
- inputs: bfloat16 [48, 2, 128, 4096], P('dp', None, None, 'tensor'), may hold values from -6 to 6
- cotangent: bfloat16 [48, 2, 128, 4096], P('dp', None, None, 'tensor'), may hold values from -6 to 6
- gate_pre: bfloat16 [48, 2, 128, 16384], P('dp', None, None, 'tensor'), may hold values from -6 to 6
- up_out: bfloat16 [48, 2, 128, 16384], P('dp', None, None, 'tensor'), may hold values from -6 to 6
- w_down: bfloat16 [16384, 4096], P('tensor'), may hold values from -0.046875 to 0.046875
- up_in_basis: bfloat16 [4096, 64], replicated, may hold values from -0.09375 to 0.09375
- up_out_basis: bfloat16 [16384, 64], P('tensor'), may hold values from -0.046875 to 0.046875
- down_in_basis: bfloat16 [16384, 64], P('tensor'), may hold values from -0.046875 to 0.046875
- down_out_basis: bfloat16 [4096, 64], replicated, may hold values from -0.09375 to 0.09375
- lengths: int32 [48, 2], P('dp'), may hold values from 32 to 128, as said below
- margins: float32 [48], P('dp'), may hold values from -4 to 4
- curvature: float32 [2, 64, 64], replicated, may hold values from 0.1 to 10
Outputs:
- train_grads: float32 [32, 2, 64, 64], P('dp', None, 'tensor')
- scores: float32 [16, 32], P(None, 'dp')
The draws below stay inside these ranges and needn't reach their ends.
Inputs may be any that keep to these rules, and one draw needn't show every extreme that they name: `lengths`: each entry counts the live tokens of a sequence; positions from it on are padding and take no part. In every draw some sequence is full and some has 32 live tokens.
All inputs are finite; a program needn't handle non-finite values.
Results may differ from the reference program's by a relative error of at most 0.0043.
Values may be sent and summed in bfloat16 or wider, within the bound.
No kernel may reach another device: no remote copies, remote signals or barrier semaphores. Data moves between devices by JAX's collectives and lax.ppermute only.
A program may use at most 128 MiB of HBM per device.

```python
import math
import jax
import jax.numpy as jnp
from jax import lax

D = 4096
FF = 16384
PROJ = 64
LEN = 128
TRAIN_DEV = 2
QUERY_DEV = 1
PAIRS = 48
TRAIN = 32
QUERIES = 16
N_DP = 16


def draw_lengths(key, part):
    key = jax.random.fold_in(key, 7)
    key_first, key_second, key_third = jax.random.split(key, 3)
    drawn = jax.random.randint(key_first, (PAIRS, 2), LEN // 4, LEN + 1)
    places = jnp.arange(PAIRS * 2, dtype=jnp.int32).reshape(PAIRS, 2)
    longest = jax.random.randint(key_second, (), 0, PAIRS * 2)
    shortest = (longest + 1 + jax.random.randint(key_third, (), 0, PAIRS * 2 - 1)) % (PAIRS * 2)
    drawn = jnp.where(places == longest, LEN, drawn)
    drawn = jnp.where(places == shortest, LEN // 4, drawn)
    return drawn.astype(jnp.int32)


def level_of(stream_key, dims, cuts, low, high):
    factor_of = 1.0
    for position, parts in cuts:
        heights = jax.random.uniform(jax.random.fold_in(jax.random.fold_in(stream_key, 6), position), (parts,), jnp.float32, low / len(cuts), high / len(cuts))
        factor_of = factor_of * jnp.repeat(jnp.exp(heights), dims[position] // parts).reshape((-1,) + (1,) * (len(dims) - 1 - position))
    return factor_of


def centred(key, dims, spread, most, shards=(), held_as=jnp.bfloat16):
    loudness = level_of(key, dims, shards, -0.22, 0.18) if shards else 1.0
    result = jax.random.normal(key, dims, jnp.float32) * spread * loudness
    return jnp.minimum(jnp.maximum(result, -most), most).astype(held_as)


def setup_inputs(seed: int = 0) -> dict:
    arg_keys = jax.random.split(jax.random.key(seed), 13)
    inputs = centred(arg_keys[0], (PAIRS, 2, LEN, D), 1.0, 6.0, ((0, 16), (3, 16)))
    cotangent = centred(arg_keys[1], (PAIRS, 2, LEN, D), 1.0, 6.0, ((0, 16), (3, 16)))
    gate_pre = centred(arg_keys[2], (PAIRS, 2, LEN, FF), 1.0, 6.0, ((0, 16), (3, 16)))
    up_out = centred(arg_keys[3], (PAIRS, 2, LEN, FF), 1.0, 6.0, ((0, 16), (3, 16)))
    w_down = centred(arg_keys[4], (FF, D), FF ** -0.5, 0.046875, ((0, 16),))
    up_in_basis = centred(arg_keys[5], (D, PROJ), D ** -0.5, 0.09375)
    up_out_basis = centred(arg_keys[6], (FF, PROJ), FF ** -0.5, 0.046875, ((0, 16),))
    down_in_basis = centred(arg_keys[7], (FF, PROJ), FF ** -0.5, 0.046875, ((0, 16),))
    down_out_basis = centred(arg_keys[8], (D, PROJ), D ** -0.5, 0.09375)
    lengths = draw_lengths(jax.random.fold_in(arg_keys[12], 71), 0)
    margins = jnp.clip(jax.random.uniform(arg_keys[10], (PAIRS,), jnp.float32, -4.0, 4.0) * level_of(arg_keys[10], (PAIRS,), ((0, 16),), -0.4, 0.0), -4.0, 4.0)
    curvature = jnp.clip(jnp.exp(jax.random.uniform(arg_keys[11], (2, PROJ, PROJ), jnp.float32, math.log(0.1), math.log(10.0))), 0.1, 10.0)
    return dict(inputs=inputs, cotangent=cotangent, gate_pre=gate_pre, up_out=up_out, w_down=w_down, up_in_basis=up_in_basis, up_out_basis=up_out_basis, down_in_basis=down_in_basis, down_out_basis=down_out_basis, lengths=lengths, margins=margins, curvature=curvature)


highest = lax.Precision.HIGHEST

def reference(inputs, cotangent, gate_pre, up_out, w_down, up_in_basis, up_out_basis, down_in_basis, down_out_basis, lengths, margins, curvature):

    def one_pair(operands):
        pair_inputs, pair_cotangent, pair_gate, pair_up, pair_lengths, pair_margin = operands
        token_count = 2 * LEN
        flat_inputs = pair_inputs.reshape(token_count, D)
        flat_cotangent = pair_cotangent.reshape(token_count, D)
        hidden_grad = jnp.dot(flat_cotangent, w_down.T, preferred_element_type=jnp.float32)
        gate_value = jax.nn.silu(pair_gate.reshape(token_count, FF).astype(jnp.float32))
        up_grad = (hidden_grad * gate_value).astype(jnp.bfloat16)
        activation = (gate_value * pair_up.reshape(token_count, FF).astype(jnp.float32)).astype(jnp.bfloat16)
        positions = jnp.arange(LEN, dtype=jnp.int32)
        live = (positions[None, :] < pair_lengths[:, None]).astype(jnp.float32).reshape(token_count, 1)
        input_proj = jnp.dot(flat_inputs, up_in_basis, preferred_element_type=jnp.float32) * live
        cotangent_proj = jnp.dot(flat_cotangent, down_out_basis, preferred_element_type=jnp.float32) * live
        up_proj = jnp.dot(up_grad, up_out_basis, preferred_element_type=jnp.float32)
        act_proj = jnp.dot(activation, down_in_basis, preferred_element_type=jnp.float32)
        input_proj = input_proj.reshape(2, LEN, PROJ)
        cotangent_proj = cotangent_proj.reshape(2, LEN, PROJ)
        up_proj = up_proj.reshape(2, LEN, PROJ)
        act_proj = act_proj.reshape(2, LEN, PROJ)
        seq_up = jnp.einsum('sti,stj->sij', input_proj, up_proj, precision=highest)
        seq_down = jnp.einsum('sti,stj->sij', act_proj, cotangent_proj, precision=highest)
        seq_grads = jnp.stack([seq_up, seq_down], axis=1)
        return (seq_grads[0] - seq_grads[1]) / (1.0 + jnp.exp(pair_margin))
    pair_grads = lax.map(one_pair, (inputs, cotangent, gate_pre, up_out, lengths, margins))
    grouped = pair_grads.reshape(N_DP, TRAIN_DEV + QUERY_DEV, 2, PROJ, PROJ)
    train_grads = grouped[:, :TRAIN_DEV].reshape(TRAIN, 2, PROJ, PROJ)
    query_grads = grouped[:, TRAIN_DEV:].reshape(QUERIES, 2, PROJ, PROJ)
    weighted = curvature[None] * train_grads
    self_terms = lax.optimization_barrier(jnp.sum(weighted * train_grads, axis=(1, 2, 3)))
    cross = jnp.dot(query_grads.reshape(QUERIES, 2 * PROJ * PROJ), weighted.reshape(TRAIN, 2 * PROJ * PROJ).T, precision=highest)
    scores = cross / jnp.sqrt(self_terms + 1e-06)[None, :]
    return (train_grads, scores)
```

```python
import jax
import jax.numpy as jnp
from jax import lax
from jax.experimental import pallas as pl
from jax.experimental.pallas import tpu as pltpu
from jax.sharding import PartitionSpec as P

QUERY_DEV = 1
NX, NY, NC = 4, 2, 2
highest = lax.Precision.HIGHEST
epsilon = 1e-06
F32, BF16 = jnp.float32, jnp.bfloat16
VMEM_LIMIT = 56 * 1024 * 1024


def moves(step):
    pairs = []
    for x in range(NX):
        for y in range(NY):
            for c in range(NC):
                tx, ty, tc = step(x, y, c)
                source = (x * NY + y) * NC + c
                target = ((tx % NX) * NY + ty % NY) * NC + tc % NC
                pairs.append((source, target))
    return pairs


X_UP = moves(lambda x, y, c: (x + 1, y, c))
X_DOWN = moves(lambda x, y, c: (x - 1, y, c))
Y_SWAP = moves(lambda x, y, c: (x, y + 1, c))
CORE_SWAP = moves(lambda x, y, c: (x, y, c + 1))


def send(value, pairs):
    return lax.ppermute(value, "tensor", pairs)


def dot_t(a, b):
    return lax.dot_general(a, b, (((1,), (1,)), ((), ())), preferred_element_type=F32)


def columns_of_core(w_down, core):
    rows = w_down.shape[0]
    chips = NX * NY
    width = w_down.shape[1] // (chips * NC)

    def body(core_ref, w_ref, o_ref):
        o_ref[...] = w_ref[...]

    return pl.pallas_call(
        body,
        grid_spec=pltpu.PrefetchScalarGridSpec(
            num_scalar_prefetch=1,
            grid=(chips,),
            in_specs=[pl.BlockSpec((rows, width), lambda i, core_ref: (0, NC * i + core_ref[0]))],
            out_specs=pl.BlockSpec((rows, width), lambda i, core_ref: (0, i)),
        ),
        out_shape=jax.ShapeDtypeStruct((rows, chips * width), w_down.dtype),
        compiler_params=pltpu.CompilerParams(vmem_limit_bytes=VMEM_LIMIT),
        name="columns_of_core",
    )(core[None], w_down)


def stage(blocks, pieces, weights, other_weights, gate, other_gate, bases, row_block, tokens, last=None):
    shards_n = len(pieces)
    width = pieces[0][0].shape[1]
    hidden = gate.shape[1]
    chunk = 512
    steps = hidden // chunk
    basis, other_basis, out_basis = bases
    flat = [piece for shard in pieces for piece in shard]
    counts = [len(shard) for shard in pieces]
    pair_tokens = 256
    pairs = tokens // pair_tokens

    def body(blocks_ref, *refs):
        refs = list(refs)
        cots = []
        for count in counts:
            got = [refs.pop(0) for _ in range(count)]
            cots.append(got)
        own_w = [refs.pop(0) for _ in range(shards_n)]
        other_w = [refs.pop(0) for _ in range(shards_n)]
        out_bases = [refs.pop(0) for _ in range(shards_n)]
        gate_ref, other_gate_ref, basis_ref, other_basis_ref = refs[:4]
        refs = refs[4:]
        if last is not None:
            before_ref, left_ref, grads_ref, sums_ref = refs
        else:
            (sums_ref,) = refs
        step = pl.program_id(0)
        values = [
            got[0][...] if len(got) == 1 else jnp.concatenate([ref[...] for ref in got], axis=0)
            for got in cots
        ]

        @pl.when(step == 0)
        def _():
            first = before_ref[...] if last is not None else jnp.zeros(sums_ref.shape, F32)
            for value, ref in zip(values, out_bases):
                first = first + jnp.dot(value, ref[...], preferred_element_type=F32)
            sums_ref[...] = first

        total = sums_ref[...]
        for w_refs, g_ref, b_ref in ((own_w, gate_ref, basis_ref), (other_w, other_gate_ref, other_basis_ref)):
            grad = dot_t(values[0], w_refs[0][...])
            for value, ref in zip(values[1:], w_refs[1:]):
                grad = grad + dot_t(value, ref[...])
            gate_value = g_ref[...].astype(F32)
            gate_value = gate_value / (1.0 + jnp.exp(-gate_value))
            total = total + jnp.dot((grad * gate_value).astype(BF16), b_ref[...], preferred_element_type=F32)
        sums_ref[...] = total

        if last is not None:

            @pl.when(step == steps - 1)
            def _():
                half = lax.broadcasted_iota(jnp.int32, (64, 128), 1) < 64
                for pair in range(pairs):
                    rows = pl.ds(pair * pair_tokens, pair_tokens)
                    both = lax.dot_general(
                        left_ref[rows, :],
                        sums_ref[rows, :],
                        (((0,), (0,)), ((), ())),
                        precision=highest,
                        preferred_element_type=F32,
                    )
                    grads_ref[pair] = jnp.where(half, both[:64], both[64:])

    def whole(array):
        return pl.BlockSpec(array.shape, lambda i, blocks_ref: (0,) * array.ndim)

    def at(row, s):
        return lambda i, blocks_ref: (i, blocks_ref[row * shards_n + s])

    in_specs = [whole(piece) for piece in flat]
    operands = list(flat)
    for s in range(shards_n):
        in_specs.append(pl.BlockSpec((chunk, width), at(0, s)))
        operands.append(weights)
    for s in range(shards_n):
        in_specs.append(pl.BlockSpec((chunk, width), at(1, s)))
        operands.append(other_weights)
    for s in range(shards_n):
        in_specs.append(
            pl.BlockSpec((width, 128), lambda i, blocks_ref, s=s: (blocks_ref[s], 0))
        )
        operands.append(out_basis)
    for array in (gate, other_gate):
        in_specs.append(pl.BlockSpec((tokens, chunk), lambda i, blocks_ref: (row_block, i)))
        operands.append(array)
    for array in (basis, other_basis):
        in_specs.append(pl.BlockSpec((chunk, 128), lambda i, blocks_ref: (i, 0)))
        operands.append(array)
    sums_spec = pl.BlockSpec((tokens, 128), lambda i, blocks_ref: (0, 0))
    sums_shape = jax.ShapeDtypeStruct((tokens, 128), F32)
    out_specs, out_shape = sums_spec, sums_shape
    scratch = []
    if last is not None:
        before, left = last
        in_specs.append(sums_spec)
        operands.append(before)
        in_specs.append(pl.BlockSpec((tokens, 128), lambda i, blocks_ref: (row_block, 0)))
        operands.append(left)
        out_specs = pl.BlockSpec((pairs, 64, 128), lambda i, blocks_ref: (0, 0, 0))
        out_shape = jax.ShapeDtypeStruct((pairs, 64, 128), F32)
        scratch = [pltpu.VMEM((tokens, 128), F32)]
    flops = 4 * tokens * hidden * (shards_n * width + 128)
    return pl.pallas_call(
        body,
        grid_spec=pltpu.PrefetchScalarGridSpec(
            num_scalar_prefetch=1,
            grid=(steps,),
            in_specs=in_specs,
            out_specs=out_specs,
            scratch_shapes=scratch,
        ),
        out_shape=out_shape,
        compiler_params=pltpu.CompilerParams(vmem_limit_bytes=VMEM_LIMIT),
        cost_estimate=pl.CostEstimate(
            flops=flops,
            bytes_accessed=4 * shards_n * width * hidden + 4 * tokens * hidden,
            transcendentals=2 * tokens * hidden,
        ),
        name="stage_last" if last is not None else "stage_first",
    )(blocks, *operands)


def pack_tokens(value):
    tokens = value.shape[0]
    return value.reshape(16, 2, tokens // 32, 64).transpose(0, 2, 1, 3).reshape(16, tokens // 32, 128)


def unpack_tokens(value):
    rows = value.shape[1]
    return value.reshape(16, rows, 2, 64).transpose(0, 2, 1, 3).reshape(rows * 32, 64)


def shards(
    inputs,
    cotangent,
    gate_pre,
    up_out,
    w_down,
    up_in_basis,
    up_out_basis,
    down_in_basis,
    down_out_basis,
    lengths,
    margins,
    curvature,
):
    pair_count = inputs.shape[0]
    seq_len = inputs.shape[2]
    width = inputs.shape[3]
    hidden = gate_pre.shape[3]
    pair_tokens = 2 * seq_len
    token_count = pair_count * pair_tokens
    train_count = pair_count - QUERY_DEV
    train_tokens = train_count * pair_tokens
    query_tokens = QUERY_DEV * pair_tokens
    dp_size = lax.axis_size("dp")
    tensor_size = lax.axis_size("tensor")
    place = lax.axis_index("tensor")
    x, y, core = place // (NY * NC), (place // NC) % NY, place % NC

    flat_cotangent = cotangent.reshape(token_count, width)
    gate = gate_pre.reshape(token_count, hidden)
    query_own = flat_cotangent[train_tokens:]
    train_own = flat_cotangent[:train_tokens]

    def first_hop(own):
        return send(own, X_UP), send(own, X_DOWN), send(own, Y_SWAP)

    def second_hop(left, across):
        return send(left, X_UP), send(across, X_DOWN), send(left, Y_SWAP)

    query_left, query_right, query_across = first_hop(query_own)
    train_left, train_right, train_across = first_hop(train_own)

    other_gate = send(gate, CORE_SWAP)
    other_weights = send(columns_of_core(w_down, 1 - core), CORE_SWAP)
    padded_basis = jnp.pad(up_out_basis, ((0, 0), (0, 64)))
    other_basis = send(padded_basis, CORE_SWAP)
    padded_out_basis = jnp.pad(down_out_basis, ((0, 0), (64, 0)))
    bases = (padded_basis, other_basis, padded_out_basis)

    rows = lax.dynamic_slice_in_dim(up_in_basis, place * width, width, 0)
    partial_inputs = jnp.dot(inputs.reshape(token_count, width), rows, preferred_element_type=F32)
    pieces = lax.all_to_all(pack_tokens(partial_inputs), "tensor", 0, 0, tiled=True)
    mine = jnp.sum(pieces, axis=0)
    spread = jnp.broadcast_to(mine[None], (tensor_size, *mine.shape))
    input_proj = unpack_tokens(lax.all_to_all(spread, "tensor", 0, 0, tiled=True))

    gate_value = jax.nn.silu(gate.astype(F32))
    activation = (gate_value * up_out.reshape(token_count, hidden).astype(F32)).astype(BF16)
    act_proj = jnp.dot(activation, down_in_basis, preferred_element_type=F32)
    act_proj = act_proj + send(act_proj, CORE_SWAP)

    positions = jnp.arange(seq_len, dtype=jnp.int32)
    live = (positions[None, None, :] < lengths[:, :, None]).astype(F32)
    weight = 1.0 / (1.0 + jnp.exp(margins))
    factor = live * weight[:, None, None] * jnp.array([1.0, -1.0], F32)[None, :, None]
    left_factors = jnp.concatenate([input_proj, act_proj], axis=1) * factor.reshape(token_count, 1)

    chip = x * NY + y
    flipped = 1 - y

    def chip_at(dx, row):
        return ((x + dx) % NX) * NY + row

    near = jnp.stack([chip, chip_at(3, y), chip_at(1, y), chip_at(0, flipped)])
    far = jnp.stack([chip_at(2, y), chip_at(1, flipped), chip_at(3, flipped), chip_at(2, flipped)])
    near_blocks = jnp.concatenate([near * NC + core, near]).astype(jnp.int32)
    far_blocks = jnp.concatenate([far * NC + core, far]).astype(jnp.int32)
    query_block = train_tokens // query_tokens

    query_x2, query_pr, query_pl = second_hop(query_left, query_across)
    train_x2, train_pr, train_pl = second_hop(train_left, train_across)

    query_near = stage(
        near_blocks,
        [(query_own,), (query_left,), (query_right,), (query_across,)],
        w_down, other_weights, gate, other_gate, bases, query_block, query_tokens,
    )
    query_far = send(query_x2, Y_SWAP)
    train_near = stage(
        near_blocks,
        [(train_own,), (train_left,), (train_right,), (train_across,)],
        w_down, other_weights, gate, other_gate, bases, 0, train_tokens,
    )
    middle = train_tokens // 2
    train_far = (send(train_pl[:middle], X_UP), send(train_pr[middle:], X_DOWN))

    query_grads = stage(
        far_blocks,
        [(query_x2,), (query_pr,), (query_pl,), (query_far,)],
        w_down, other_weights, gate, other_gate, bases, query_block, query_tokens,
        (query_near, left_factors),
    )
    row_share = 64 // tensor_size
    query_out = jnp.broadcast_to(
        query_grads.reshape(1, tensor_size, row_share, 128), (dp_size, tensor_size, row_share, 128)
    ).reshape(dp_size * tensor_size, row_share, 128)
    query_parts = lax.all_to_all(query_out, ("dp", "tensor"), 0, 0, tiled=True)

    train_grads = stage(
        far_blocks,
        [(train_x2,), (train_pr,), (train_pl,), train_far],
        w_down, other_weights, gate, other_gate, bases, 0, train_tokens,
        (train_near, left_factors),
    )
    train_out = train_grads.reshape(train_count, tensor_size, row_share, 128).transpose(1, 0, 2, 3)
    train_parts = lax.all_to_all(
        train_out.reshape(tensor_size, train_count * row_share, 128), "tensor", 0, 0, tiled=True
    )
    train_rows = jnp.sum(train_parts, axis=0).reshape(train_count, row_share, 128)
    query_rows = jnp.sum(query_parts.reshape(dp_size, tensor_size, row_share, 128), axis=1)

    own_curvature = lax.dynamic_slice_in_dim(curvature, place * row_share, row_share, 1)
    own_curvature = own_curvature.transpose(1, 0, 2).reshape(row_share, 128)
    weighted = own_curvature[None] * train_rows
    self_part = jnp.sum(weighted * train_rows, axis=(1, 2))
    cross_part = jnp.sum(query_rows[:, None] * weighted[None], axis=(2, 3))
    sums = jnp.concatenate([cross_part.reshape(-1), self_part])
    sums = jnp.pad(sums, (0, 128 - sums.shape[0]))
    all_sums = lax.all_to_all(
        jnp.broadcast_to(sums[None, None], (tensor_size, 1, 128)), "tensor", 0, 0, tiled=True
    )
    sums = jnp.sum(all_sums, axis=(0, 1))
    cross = sums[: dp_size * train_count].reshape(dp_size, train_count)
    self_terms = sums[dp_size * train_count : dp_size * train_count + train_count]
    scores = cross / jnp.sqrt(self_terms + epsilon)[None, :]
    train_block = train_rows.reshape(train_count, row_share, 2, 64).transpose(0, 2, 1, 3)
    return train_block, scores


def solution(mesh):
    return jax.shard_map(
        shards,
        mesh=mesh,
        in_specs=(
            P("dp", None, None, "tensor"),
            P("dp", None, None, "tensor"),
            P("dp", None, None, "tensor"),
            P("dp", None, None, "tensor"),
            P("tensor", None),
            P(),
            P("tensor", None),
            P("tensor", None),
            P(),
            P("dp", None),
            P("dp"),
            P(),
        ),
        out_specs=(P("dp", None, "tensor", None), P(None, "dp")),
        check_vma=False,
    )
```

```python
import jax
import jax.numpy as jnp
from jax import lax
from jax.experimental import pallas as pl
from jax.experimental.pallas import tpu as pltpu
from jax.sharding import PartitionSpec as P

QUERY_DEV = 1
NX, NY, NC = 4, 2, 2
CHIPS = NX * NY
PROJ = 64
LANES = 128
highest = lax.Precision.HIGHEST
epsilon = 1e-06
F32, BF16 = jnp.float32, jnp.bfloat16
VMEM_LIMIT = 24 * 1024 * 1024


def moves(step):
    pairs = []
    for x in range(NX):
        for y in range(NY):
            for c in range(NC):
                tx, ty, tc = step(x, y, c)
                source = (x * NY + y) * NC + c
                target = ((tx % NX) * NY + ty % NY) * NC + tc % NC
                pairs.append((source, target))
    return pairs


X_UP = moves(lambda x, y, c: (x + 1, y, c))
X_DOWN = moves(lambda x, y, c: (x - 1, y, c))
Y_SWAP = moves(lambda x, y, c: (x, y + 1, c))
CORE_SWAP = moves(lambda x, y, c: (x, y, c + 1))
Y_OR_X = moves(lambda x, y, c: (x + c, y + 1 - c, c))

VMEM = pl.BlockSpec(memory_space=pltpu.VMEM)
ANY = pl.BlockSpec(memory_space=pl.ANY)
SMEM = pl.BlockSpec(memory_space=pltpu.SMEM)
PARAMS = pltpu.CompilerParams(vmem_limit_bytes=VMEM_LIMIT)


def send(value, pairs):
    return lax.ppermute(value, "tensor", pairs)


def dot_rows(a, b, precision=None):
    return lax.dot_general(a, b, (((0,), (0,)), ((), ())), precision=precision, preferred_element_type=F32)


def dot_t(a, b, precision=None):
    return lax.dot_general(a, b, (((1,), (1,)), ((), ())), precision=precision, preferred_element_type=F32)


def in_hbm(array):
    return pltpu.with_memory_space_constraint(array, pltpu.HBM)


def in_vmem(array):
    return pltpu.with_memory_space_constraint(array, pltpu.VMEM)


def first(place, flat, inputs, in_basis_t):
    tokens, width = flat.shape

    def body(place_ref, ref, in_ref, basis_ref, own_ref, proj_ref):
        own_ref[...] = ref[...].T
        proj_ref[...] = dot_t(basis_ref[...], in_ref[...])

    def whole(shape):
        return pl.BlockSpec(shape, lambda i, place_ref: (0, 0))

    return pl.pallas_call(
        body,
        grid_spec=pltpu.PrefetchScalarGridSpec(
            num_scalar_prefetch=1,
            grid=(1,),
            in_specs=[
                whole((tokens, width)),
                whole((tokens, width)),
                pl.BlockSpec((PROJ, width), lambda i, place_ref: (0, place_ref[0])),
            ],
            out_specs=(whole((width, tokens)), whole((PROJ, tokens))),
        ),
        out_shape=(
            jax.ShapeDtypeStruct((width, tokens), BF16),
            jax.ShapeDtypeStruct((PROJ, tokens), F32),
        ),
        compiler_params=PARAMS,
        name="first",
    )(place, in_hbm(flat), in_hbm(inputs), in_hbm(in_basis_t))


def prepare(gate, up_out, down_in_basis_t):
    tokens, hidden = gate.shape
    block = 128

    def body(gate_ref, up_ref, down_ref, g_ref, act_ref):
        raw = gate_ref[...]
        value = raw.astype(F32)
        value = value / (1.0 + jnp.exp(-value))
        activation = (value * up_ref[...].astype(F32)).astype(BF16)
        act_ref[...] = dot_t(down_ref[...], activation)
        g_ref[...] = raw.T

    return pl.pallas_call(
        body,
        grid=(tokens // block,),
        in_specs=[
            pl.BlockSpec((block, hidden), lambda i: (i, 0)),
            pl.BlockSpec((block, hidden), lambda i: (i, 0)),
            pl.BlockSpec((PROJ, hidden), lambda i: (0, 0)),
        ],
        out_specs=(
            pl.BlockSpec((hidden, block), lambda i: (0, i)),
            pl.BlockSpec((PROJ, block), lambda i: (0, i)),
        ),
        out_shape=(
            jax.ShapeDtypeStruct((hidden, tokens), BF16),
            jax.ShapeDtypeStruct((PROJ, tokens), F32),
        ),
        compiler_params=PARAMS,
        name="prepare",
    )(in_hbm(gate), in_hbm(up_out), in_hbm(down_in_basis_t))


def spread_inputs(core, proj, other_proj, copies, after):
    half = proj.shape[1] // 2

    def body(core_ref, proj_ref, other_ref, *refs):
        o_ref = refs[-1]
        start = pl.multiple_of(core_ref[0] * half, half)
        both = (proj_ref[:, pl.ds(start, half)] + other_ref[:, pl.ds(start, half)]).astype(BF16)
        for i in range(copies):
            o_ref[i] = both

    return pl.pallas_call(
        body,
        in_specs=[SMEM, VMEM, VMEM] + [ANY] * len(after),
        out_specs=VMEM,
        out_shape=jax.ShapeDtypeStruct((copies, PROJ, half), BF16),
        compiler_params=PARAMS,
        name="spread_inputs",
    )(core, proj, other_proj, *[in_hbm(array) for array in after])


def left_factors(lengths, weights, parts, act, seq_len):
    tokens = act.shape[1]
    half = tokens // 2
    sequences = tokens // seq_len

    def body(lengths_ref, weights_ref, parts_ref, act_ref, o_ref):
        lane = lax.broadcasted_iota(jnp.int32, (1, seq_len), 1)
        for c in range(NC):
            proj = parts_ref[c].astype(F32)
            for chip in range(1, CHIPS):
                proj = proj + parts_ref[chip * NC + c].astype(F32)
            o_ref[:PROJ, c * half : (c + 1) * half] = proj
        o_ref[PROJ:, :] = act_ref[...]
        for s in range(sequences):
            columns = slice(s * seq_len, (s + 1) * seq_len)
            sign = 1.0 if s % 2 == 0 else -1.0
            factor = jnp.where(lane < lengths_ref[s // 2, s % 2], weights_ref[s // 2] * sign, 0.0)
            o_ref[:, columns] = o_ref[:, columns] * factor

    return pl.pallas_call(
        body,
        in_specs=[SMEM, SMEM, VMEM, VMEM],
        out_specs=VMEM,
        out_shape=jax.ShapeDtypeStruct((2 * PROJ, tokens), F32),
        compiler_params=PARAMS,
        name="left_factors",
    )(lengths, weights, parts, act)


def stage(core, chips, mine, twins, weights, gate_t, basis_t, out_basis_t, after=(), last=None):
    width, tokens = mine[0].shape
    hidden = gate_t.shape[0]
    count = len(mine)
    depth = NC * count * width
    chunk, block = 512, 256
    steps = hidden // chunk
    pieces = [piece for pair in zip(mine, twins) for piece in pair]

    def body(core_ref, chips_ref, *refs):
        refs = list(refs)
        piece_refs = [refs.pop(0) for _ in pieces]
        w_hbm, g_hbm, b_ref, out_basis_ref = [refs.pop(0) for _ in range(4)]
        if last is not None:
            before_ref, left_ref = refs.pop(0), refs.pop(0)
        refs = refs[len(after) :]
        o_ref, cat, w_ref, g_ref, sem, w_sem, g_sem = refs[:7]
        sums = o_ref if last is None else refs[7]
        copies = []
        for i, ref in enumerate(piece_refs):
            side = core_ref[0] if i % NC == 0 else 1 - core_ref[0]
            row = pl.multiple_of((i // NC * NC + side) * width, width)
            copies.append(pltpu.make_async_copy(ref, cat.at[pl.ds(row, width)], sem.at[i]))
        weight_copies = []
        for step in range(steps):
            span = pl.ds(step * chunk, chunk)
            group = []
            for i in range(count):
                columns = pl.ds(pl.multiple_of(chips_ref[i] * NC * width, NC * width), NC * width)
                target = w_ref.at[span, pl.ds(i * NC * width, NC * width)]
                group.append(pltpu.make_async_copy(w_hbm.at[span, columns], target, w_sem.at[step, i]))
            group.append(pltpu.make_async_copy(g_hbm.at[span], g_ref.at[span], g_sem.at[step]))
            weight_copies.append(group)
        for copy in copies + weight_copies[0]:
            copy.start()
        for group in weight_copies[1:]:
            for copy in group:
                copy.start()
        out_basis = jnp.concatenate(
            [
                out_basis_ref[:, pl.ds(pl.multiple_of(chips_ref[i] * NC * width, NC * width), NC * width)]
                for i in range(count)
            ],
            axis=1,
        )
        if last is not None:
            sums[...] = before_ref[...]
        else:
            sums[...] = jnp.zeros_like(sums)
        for copy in copies:
            copy.wait()
        sums[PROJ:, :] += jnp.dot(out_basis, cat[...], preferred_element_type=F32)
        for step in range(steps):
            for copy in weight_copies[step]:
                copy.wait()
            h = step * chunk
            for t in range(0, tokens, block):
                span = slice(t, t + block)
                grad = jnp.dot(w_ref[h : h + chunk, :], cat[:, span], preferred_element_type=F32)
                gate = g_ref[h : h + chunk, span].astype(F32)
                gate = gate / (1.0 + jnp.exp(-gate))
                sums[:PROJ, span] += jnp.dot(
                    b_ref[:, h : h + chunk], (grad * gate).astype(BF16), preferred_element_type=F32
                )
        if last is not None:
            pair_tokens, devices = last[2:]
            share = PROJ // devices
            half = lax.broadcasted_iota(jnp.int32, (PROJ, LANES), 1) < PROJ
            for pair in range(tokens // pair_tokens):
                span = slice(pair * pair_tokens, (pair + 1) * pair_tokens)
                both = dot_t(left_ref[:, span], sums[:, span], highest)
                grads = jnp.where(half, both[:PROJ], both[PROJ:])
                for k in range(devices):
                    o_ref[k, pair] = grads[k * share : (k + 1) * share, :]

    operands = [core, chips, *[in_hbm(piece) for piece in pieces], in_hbm(weights), in_hbm(gate_t)]
    operands += [basis_t, out_basis_t]
    in_specs = [SMEM, SMEM] + [ANY] * (len(pieces) + 2) + [VMEM] * 2
    scratch = [
        pltpu.VMEM((depth, tokens), BF16),
        pltpu.VMEM((hidden, depth), BF16),
        pltpu.VMEM((hidden, tokens), BF16),
        pltpu.SemaphoreType.DMA((len(pieces),)),
        pltpu.SemaphoreType.DMA((steps, count)),
        pltpu.SemaphoreType.DMA((steps,)),
    ]
    shape = (2 * PROJ, tokens)
    if last is not None:
        operands += last[:2]
        in_specs += [VMEM, VMEM]
        scratch.append(pltpu.VMEM(shape, F32))
        shape = (last[3], tokens // last[2], PROJ // last[3], LANES)
    operands += [in_hbm(array) for array in after]
    in_specs += [ANY] * len(after)
    return pl.pallas_call(
        body,
        in_specs=in_specs,
        out_specs=VMEM,
        out_shape=jax.ShapeDtypeStruct(shape, F32),
        scratch_shapes=scratch,
        compiler_params=PARAMS,
        cost_estimate=pl.CostEstimate(
            flops=2 * tokens * hidden * (depth + LANES),
            bytes_accessed=2 * depth * tokens,
            transcendentals=2 * tokens * hidden,
        ),
        name="stage_last" if last is not None else "stage_first",
    )(*operands)


def shards(
    inputs,
    cotangent,
    gate_pre,
    up_out,
    w_down,
    up_in_basis,
    up_out_basis,
    down_in_basis,
    down_out_basis,
    lengths,
    margins,
    curvature,
):
    pair_count = inputs.shape[0]
    seq_len = inputs.shape[2]
    width = inputs.shape[3]
    hidden = gate_pre.shape[3]
    token_count = pair_count * 2 * seq_len
    train_count = pair_count - QUERY_DEV
    dp_size = lax.axis_size("dp")
    tensor_size = lax.axis_size("tensor")
    row_share = PROJ // tensor_size
    place = lax.axis_index("tensor")
    x, y, core = place // (NY * NC), (place // NC) % NY, place % NC

    own, proj = first(
        place[None],
        cotangent.reshape(token_count, width),
        inputs.reshape(token_count, width),
        up_in_basis.T,
    )
    other_proj = send(proj, CORE_SWAP)
    left_own, right_own, across = send(own, X_UP), send(own, X_DOWN), send(own, Y_SWAP)
    near = [own, left_own, right_own, across]
    gate_t, act = prepare(
        gate_pre.reshape(token_count, hidden),
        up_out.reshape(token_count, hidden),
        down_in_basis.T,
    )
    left_own, across, gate_t = lax.optimization_barrier((left_own, across, gate_t))
    x2, pr, pl_ = send(left_own, X_UP), send(across, X_DOWN), send(left_own, Y_SWAP)
    spread = spread_inputs(core[None], proj, other_proj, tensor_size, (left_own, right_own, across, gate_t))
    third, spread = lax.optimization_barrier((jnp.where(core == 0, x2, pl_), spread))
    parts = lax.all_to_all(spread, "tensor", 0, 0, tiled=True)
    last_hop = send(third, Y_OR_X)
    far = [x2, pr, pl_, last_hop]
    near_twins = [send(piece, CORE_SWAP) for piece in near]
    far_twins = [send(piece, CORE_SWAP) for piece in far]

    def chip_at(dx, row):
        return ((x + dx) % NX) * NY + row

    near_chips = [chip_at(0, y), chip_at(3, y), chip_at(1, y), chip_at(0, 1 - y)]
    far_chips = [chip_at(2, y), chip_at(1, 1 - y), chip_at(3, 1 - y), chip_at(2, 1 - y)]
    chips = jnp.stack(near_chips + far_chips).astype(jnp.int32)
    pair_weights = 1.0 / (1.0 + jnp.exp(margins))
    left = left_factors(lengths, pair_weights, parts, act, seq_len)
    shared = (w_down, gate_t, up_out_basis.T, down_out_basis.T)
    near_sums = stage(core[None], chips[:4], near, near_twins, *shared, after=(x2, pr, pl_))
    grads = stage(
        core[None], chips[4:], far, far_twins, *shared,
        last=(near_sums, left, 2 * seq_len, tensor_size),
    )
    grad_parts = lax.all_to_all(grads, "tensor", 0, 0, tiled=True)
    rows = jnp.sum(grad_parts, axis=0)
    train_rows, query_rows = rows[:train_count], rows[train_count:]
    query_all = lax.all_to_all(
        jnp.broadcast_to(query_rows, (dp_size, row_share, LANES)), "dp", 0, 0, tiled=True
    )

    own_curvature = lax.dynamic_slice_in_dim(curvature, place * row_share, row_share, 1)
    own_curvature = own_curvature.transpose(1, 0, 2).reshape(row_share, LANES)
    weighted = own_curvature[None] * train_rows
    self_part = jnp.sum(weighted * train_rows, axis=(1, 2))
    cross_part = jnp.sum(query_all[:, None] * weighted[None], axis=(2, 3))
    sums = jnp.concatenate([cross_part.reshape(-1), self_part])
    sums = jnp.pad(sums, (0, LANES - sums.shape[0]))
    all_sums = lax.all_to_all(
        jnp.broadcast_to(sums[None, None], (tensor_size, 1, LANES)), "tensor", 0, 0, tiled=True
    )
    sums = jnp.sum(all_sums, axis=(0, 1))
    cross = sums[: dp_size * train_count].reshape(dp_size, train_count)
    self_terms = sums[dp_size * train_count : dp_size * train_count + train_count]
    scores = cross / jnp.sqrt(self_terms + epsilon)[None, :]
    train_block = train_rows.reshape(train_count, row_share, 2, PROJ).transpose(0, 2, 1, 3)
    return train_block, scores


def solution(mesh):
    return jax.shard_map(
        shards,
        mesh=mesh,
        in_specs=(
            P("dp", None, None, "tensor"),
            P("dp", None, None, "tensor"),
            P("dp", None, None, "tensor"),
            P("dp", None, None, "tensor"),
            P("tensor", None),
            P(),
            P("tensor", None),
            P("tensor", None),
            P(),
            P("dp", None),
            P("dp"),
            P(),
        ),
        out_specs=(P("dp", None, "tensor", None), P(None, "dp")),
        check_vma=False,
    )
```

```python
import jax
import jax.numpy as jnp
from jax import lax
from jax.experimental import pallas as pl
from jax.experimental.pallas import tpu as pltpu
from jax.sharding import PartitionSpec as P

QUERY_DEV = 1
NX, NY, NC = 4, 2, 2
CHIPS = NX * NY
PROJ = 64
LANES = 128
highest = lax.Precision.HIGHEST
epsilon = 1e-06
F32, BF16 = jnp.float32, jnp.bfloat16
VMEM_LIMIT = 24 * 1024 * 1024


def moves(step):
    pairs = []
    for x in range(NX):
        for y in range(NY):
            for c in range(NC):
                tx, ty, tc = step(x, y, c)
                source = (x * NY + y) * NC + c
                target = ((tx % NX) * NY + ty % NY) * NC + tc % NC
                pairs.append((source, target))
    return pairs


X_UP = moves(lambda x, y, c: (x + 1, y, c))
X_DOWN = moves(lambda x, y, c: (x - 1, y, c))
Y_SWAP = moves(lambda x, y, c: (x, y + 1, c))
CORE_SWAP = moves(lambda x, y, c: (x, y, c + 1))
Y_OR_X = moves(lambda x, y, c: (x + c, y + 1 - c, c))

VMEM = pl.BlockSpec(memory_space=pltpu.VMEM)
ANY = pl.BlockSpec(memory_space=pl.ANY)
SMEM = pl.BlockSpec(memory_space=pltpu.SMEM)
PARAMS = pltpu.CompilerParams(vmem_limit_bytes=VMEM_LIMIT)


def send(value, pairs):
    return lax.ppermute(value, "tensor", pairs)


def dot_rows(a, b, precision=None):
    return lax.dot_general(a, b, (((0,), (0,)), ((), ())), precision=precision, preferred_element_type=F32)


def dot_t(a, b, precision=None):
    return lax.dot_general(a, b, (((1,), (1,)), ((), ())), precision=precision, preferred_element_type=F32)


def in_hbm(array):
    return pltpu.with_memory_space_constraint(array, pltpu.HBM)


def in_vmem(array):
    return pltpu.with_memory_space_constraint(array, pltpu.VMEM)


def first(place, flat, inputs, in_basis_t):
    tokens, width = flat.shape

    def body(place_ref, ref, in_ref, basis_ref, own_ref):
        own_ref[:width, :] = ref[...].T
        own_ref[width:, :] = dot_t(basis_ref[...], in_ref[...]).astype(BF16)

    def whole(shape):
        return pl.BlockSpec(shape, lambda i, place_ref: (0, 0))

    shape = (width + PROJ, tokens)
    return pl.pallas_call(
        body,
        grid_spec=pltpu.PrefetchScalarGridSpec(
            num_scalar_prefetch=1,
            grid=(1,),
            in_specs=[
                whole((tokens, width)),
                whole((tokens, width)),
                pl.BlockSpec((PROJ, width), lambda i, place_ref: (0, place_ref[0])),
            ],
            out_specs=whole(shape),
        ),
        out_shape=jax.ShapeDtypeStruct(shape, BF16),
        compiler_params=PARAMS,
        name="first",
    )(place, in_hbm(flat), in_hbm(inputs), in_hbm(in_basis_t))


def prepare(gate, up_out, down_in_basis_t):
    tokens, hidden = gate.shape
    block = tokens // 2

    def body(gate_ref, up_ref, down_ref, g_ref, act_ref):
        raw = gate_ref[...]
        value = raw.astype(F32)
        value = value / (1.0 + jnp.exp(-value))
        activation = (value * up_ref[...].astype(F32)).astype(BF16)
        act_ref[...] = dot_t(down_ref[...], activation)
        g_ref[...] = raw.T

    return pl.pallas_call(
        body,
        grid=(tokens // block,),
        in_specs=[
            pl.BlockSpec((block, hidden), lambda i: (i, 0)),
            pl.BlockSpec((block, hidden), lambda i: (i, 0)),
            pl.BlockSpec((PROJ, hidden), lambda i: (0, 0)),
        ],
        out_specs=(
            pl.BlockSpec((hidden, block), lambda i: (0, i)),
            pl.BlockSpec((PROJ, block), lambda i: (0, i)),
        ),
        out_shape=(
            pltpu.VMEM((hidden, tokens), BF16),
            jax.ShapeDtypeStruct((PROJ, tokens), F32),
        ),
        compiler_params=PARAMS,
        name="prepare",
    )(in_hbm(gate), in_hbm(up_out), in_hbm(down_in_basis_t))


class Stage:
    chunk = 256
    block = 256

    def __init__(self, count, width, hidden, tokens):
        self.count, self.width, self.hidden, self.tokens = count, width, hidden, tokens
        self.steps, self.blocks = hidden // self.chunk, tokens // self.block
        self.depth = NC * count * width
        self.weights_shape = (PROJ + hidden, self.depth)

    def scratch(self):
        pieces = NC * self.count
        return [
            pltpu.VMEM((self.depth, self.tokens), BF16),
            pltpu.VMEM((pieces * PROJ, self.tokens), BF16),
            pltpu.VMEM((self.hidden, self.tokens), BF16),
            pltpu.SemaphoreType.DMA((self.blocks + 1, pieces)),
        ]

    def feature_copies(self, core, refs, cat, proj, sem):
        groups = [[] for _ in range(self.blocks + 1)]
        width, block = self.width, self.block
        for i, ref in enumerate(refs):
            side = core if i % NC == 0 else 1 - core
            row = pl.multiple_of((i // NC * NC + side) * width, width)
            for t in range(self.blocks):
                span = pl.ds(t * block, block)
                target = cat.at[pl.ds(row, width), span]
                groups[t].append(pltpu.make_async_copy(ref.at[pl.ds(0, width), span], target, sem.at[t, i]))
            target = proj.at[pl.ds(i * PROJ, PROJ)]
            source = ref.at[pl.ds(width, PROJ)]
            groups[-1].append(pltpu.make_async_copy(source, target, sem.at[self.blocks, i]))
        return groups

    def weight_copies(self, chips_ref, first_chip, w_hbm, out_hbm, w_ref, sem):
        wide = NC * self.width
        groups = [[] for _ in range(self.steps)]
        for i in range(self.count):
            source = pl.ds(pl.multiple_of(chips_ref[first_chip + i] * wide, wide), wide)
            target = pl.ds(i * wide, wide)
            groups[0].append(
                pltpu.make_async_copy(
                    out_hbm.at[:, source], w_ref.at[pl.ds(0, PROJ), target], sem.at[self.steps, i]
                )
            )
            for step in range(self.steps):
                rows = pl.ds(step * self.chunk, self.chunk)
                to_rows = pl.ds(PROJ + step * self.chunk, self.chunk)
                groups[step].append(
                    pltpu.make_async_copy(w_hbm.at[rows, source], w_ref.at[to_rows, target], sem.at[step, i])
                )
        return groups

    def weight_semaphores(self):
        return pltpu.SemaphoreType.DMA((self.steps + 1, self.count))

    def span(self, t):
        return slice(t * self.block, (t + 1) * self.block)

    def dots(self, step, t, w_ref, g_ref, cat, scaled):
        h, span = step * self.chunk, self.span(t)
        skip = PROJ if step == 0 else 0
        rows = slice(PROJ + h - skip, PROJ + h + self.chunk)
        grad = jnp.dot(w_ref[rows, :], cat[:, span], preferred_element_type=F32)
        gate = g_ref[h : h + self.chunk, span].astype(F32)
        gate = gate / (1.0 + jnp.exp(-gate))
        scaled[h : h + self.chunk, span] = (grad[skip:] * gate).astype(BF16)
        return grad[:skip]

    def projections(self, proj):
        total = proj[:PROJ, :].astype(F32)
        for i in range(1, NC * self.count):
            total = total + proj[i * PROJ : (i + 1) * PROJ, :].astype(F32)
        return total

    def cost(self):
        return pl.CostEstimate(
            flops=2 * self.tokens * self.hidden * (self.depth + LANES),
            bytes_accessed=2 * self.depth * (self.tokens + self.hidden),
            transcendentals=2 * self.tokens * self.hidden,
        )


def start(copies):
    for copy in copies:
        copy.start()


def wait(copies):
    for copy in copies:
        copy.wait()


def middle_stage(core, chips, first_chip, pieces, weights, gates, basis_t, out_basis_t, before=None, next_chips=0):
    count = len(pieces) // NC
    height, tokens = pieces[0].shape
    hidden = gates.shape[0]
    plan = Stage(count, height - PROJ, hidden, tokens)
    follow = Stage(next_chips, height - PROJ, hidden, tokens)

    def body(core_ref, chips_ref, *refs):
        refs = list(refs)
        piece_refs = [refs.pop(0) for _ in pieces]
        w_hbm, out_hbm, g_ref, b_ref = [refs.pop(0) for _ in range(4)]
        before_ref = refs.pop(0) if before is not None else None
        sums = refs.pop(0)
        next_ref = refs.pop(0) if next_chips else None
        cat, proj, scaled, sem, w_ref, w_sem = refs[:6]
        features = plan.feature_copies(core_ref[0], piece_refs, cat, proj, sem)
        columns = plan.weight_copies(chips_ref, first_chip, w_hbm, out_hbm, w_ref, w_sem)
        more = []
        if next_chips:
            more = follow.weight_copies(chips_ref, first_chip + count, w_hbm, out_hbm, next_ref, refs[6])
        groups = [(features[i] if i < plan.blocks else []) + columns[i] for i in range(plan.steps)]
        start(groups[0])
        start(groups[1])
        for i in range(plan.steps):
            wait(groups[i])
            if i + 2 < plan.steps:
                start(groups[i + 2])
            elif i + 2 == plan.steps:
                start(features[-1])
                for group in more:
                    start(group)
            for step in range(i + 1):
                for t in range(min(i + 1, plan.blocks)):
                    if step == i or t == i:
                        down = plan.dots(step, t, w_ref, g_ref, cat, scaled)
                        if step == 0:
                            rows = slice(PROJ, 2 * PROJ)
                            if before_ref is not None:
                                down = down + before_ref[rows, plan.span(t)]
                            sums[rows, plan.span(t)] = down
        for t in range(plan.blocks):
            span = plan.span(t)
            up = jnp.dot(b_ref[...], scaled[:, span], preferred_element_type=F32)
            if before_ref is not None:
                up = up + before_ref[:PROJ, span]
            sums[:PROJ, span] = up
        wait(features[-1])
        total = plan.projections(proj)
        if before_ref is not None:
            total = total + before_ref[2 * PROJ :, :]
        sums[2 * PROJ :, :] = total
        for group in more:
            wait(group)

    operands = [core, chips, *[in_hbm(piece) for piece in pieces], in_hbm(weights), in_hbm(out_basis_t)]
    operands += [in_vmem(gates), basis_t]
    in_specs = [SMEM, SMEM] + [ANY] * (len(pieces) + 2) + [VMEM, VMEM]
    scratch = plan.scratch() + [pltpu.VMEM(plan.weights_shape, BF16), plan.weight_semaphores()]
    out_specs, out_shape = [VMEM], [jax.ShapeDtypeStruct((3 * PROJ, tokens), F32)]
    if before is not None:
        operands.append(before)
        in_specs.append(VMEM)
    if next_chips:
        out_specs.append(VMEM)
        out_shape.append(pltpu.VMEM(follow.weights_shape, BF16))
        scratch.append(follow.weight_semaphores())
    return pl.pallas_call(
        body,
        in_specs=in_specs,
        out_specs=out_specs,
        out_shape=out_shape,
        scratch_shapes=scratch,
        compiler_params=PARAMS,
        cost_estimate=plan.cost(),
        name="middle_stage",
    )(*operands)


def last_stage(core, lengths, pair_weights, pieces, near, weights, gates, basis_t, act, seq_len, devices):
    count = len(pieces) // NC
    height, tokens = pieces[0].shape
    hidden = gates.shape[0]
    plan = Stage(count, height - PROJ, hidden, tokens)
    pair_tokens = 2 * seq_len
    pairs = tokens // pair_tokens
    share = PROJ // devices

    def body(core_ref, lengths_ref, pair_ref, *refs):
        piece_refs, refs = refs[: len(pieces)], refs[len(pieces) :]
        near_ref, w_ref, g_ref, b_ref, act_ref, o_ref, cat, proj, scaled, sem, left, sums = refs
        features = plan.feature_copies(core_ref[0], piece_refs, cat, proj, sem)
        start(features[0])
        start(features[1])
        for t in range(plan.blocks):
            wait(features[t])
            if t + 2 <= plan.blocks:
                start(features[t + 2])
            span = plan.span(t)
            for step in range(plan.steps):
                down = plan.dots(step, t, w_ref, g_ref, cat, scaled)
                if step == 0:
                    sums[PROJ:, span] = down + near_ref[PROJ : 2 * PROJ, span]
            up = jnp.dot(b_ref[...], scaled[:, span], preferred_element_type=F32)
            sums[:PROJ, span] = up + near_ref[:PROJ, span]
        wait(features[-1])
        left[:PROJ, :] = plan.projections(proj) + near_ref[2 * PROJ :, :]
        left[PROJ:, :] = act_ref[...]
        lane = lax.broadcasted_iota(jnp.int32, (1, seq_len), 1)
        for s in range(tokens // seq_len):
            columns = slice(s * seq_len, (s + 1) * seq_len)
            sign = 1.0 if s % 2 == 0 else -1.0
            factor = jnp.where(lane < lengths_ref[s // 2, s % 2], pair_ref[s // 2] * sign, 0.0)
            left[:, columns] = left[:, columns] * factor
        half = lax.broadcasted_iota(jnp.int32, (PROJ, LANES), 1) < PROJ
        for pair in range(pairs):
            span = slice(pair * pair_tokens, (pair + 1) * pair_tokens)
            both = dot_t(left[:, span], sums[:, span], highest)
            grads = jnp.where(half, both[:PROJ], both[PROJ:])
            grads = grads.astype(BF16).reshape(devices, share, LANES)
            for c in range(NC):
                mine = jnp.concatenate([grads[k] for k in range(c, devices, NC)], axis=0)
                for k in range(c, devices, NC):
                    o_ref[k, pair * PROJ // NC : (pair + 1) * PROJ // NC, :] = mine

    return pl.pallas_call(
        body,
        in_specs=[SMEM, SMEM, SMEM] + [ANY] * len(pieces) + [VMEM] * 5,
        out_specs=VMEM,
        out_shape=jax.ShapeDtypeStruct((devices, pairs * PROJ // NC, LANES), BF16),
        scratch_shapes=plan.scratch()
        + [pltpu.VMEM((2 * PROJ, tokens), F32), pltpu.VMEM((2 * PROJ, tokens), F32)],
        compiler_params=PARAMS,
        cost_estimate=plan.cost(),
        name="last_stage",
    )(
        core, lengths, pair_weights, *[in_hbm(piece) for piece in pieces],
        near, in_vmem(weights), in_vmem(gates), basis_t, act,
    )


def shards(
    inputs,
    cotangent,
    gate_pre,
    up_out,
    w_down,
    up_in_basis,
    up_out_basis,
    down_in_basis,
    down_out_basis,
    lengths,
    margins,
    curvature,
):
    pair_count = inputs.shape[0]
    seq_len = inputs.shape[2]
    width = inputs.shape[3]
    hidden = gate_pre.shape[3]
    token_count = pair_count * 2 * seq_len
    train_count = pair_count - QUERY_DEV
    dp_size = lax.axis_size("dp")
    tensor_size = lax.axis_size("tensor")
    row_share = PROJ // tensor_size
    place = lax.axis_index("tensor")
    x, y, core = place // (NY * NC), (place // NC) % NY, place % NC

    own = first(
        place[None],
        cotangent.reshape(token_count, width),
        inputs.reshape(token_count, width),
        up_in_basis.T,
    )
    gates, act = prepare(
        gate_pre.reshape(token_count, hidden),
        up_out.reshape(token_count, hidden),
        down_in_basis.T,
    )
    pair_weights = 1.0 / (1.0 + jnp.exp(margins))

    def chip_at(dx, row):
        return ((x + dx) % NX) * NY + row

    flip = 1 - y
    near_chips = [chip_at(0, y), chip_at(3, y), chip_at(1, y), chip_at(0, flip)]
    far_chips = [chip_at(2, y), chip_at(1, flip), chip_at(3, flip), chip_at(2, flip)]
    chips = jnp.stack(near_chips + far_chips).astype(jnp.int32)
    bases = (up_out_basis.T, down_out_basis.T)

    def with_twins(pieces):
        return [shard for piece in pieces for shard in (piece, send(piece, CORE_SWAP))]

    near = (send(own, X_UP), send(own, X_DOWN), send(own, Y_SWAP))
    (sums,) = middle_stage(core[None], chips, 0, with_twins([own]), w_down, gates, *bases)
    left_own, first_sums = lax.optimization_barrier((near[0], sums))
    right_own, across, sums = lax.optimization_barrier((*near[1:], first_sums))
    near = (left_own, right_own, across)
    x2, pr, pl_ = send(left_own, X_UP), send(across, X_DOWN), send(left_own, Y_SWAP)
    (sums,) = middle_stage(core[None], chips, 1, with_twins(near), w_down, gates, *bases, before=sums)
    third, far, sums = lax.optimization_barrier((jnp.where(core == 0, x2, pl_), (x2, pr, pl_), sums))
    last_hop = send(third, Y_OR_X)
    sums, last_weights = middle_stage(
        core[None], chips, 4, with_twins(far), w_down, gates, *bases, before=sums, next_chips=1
    )
    last_hop, sums = lax.optimization_barrier((last_hop, sums))
    grads = last_stage(
        core[None], lengths, pair_weights, with_twins([last_hop]),
        sums, last_weights, gates, up_out_basis.T, act, seq_len, tensor_size,
    )
    grad_parts = lax.all_to_all(grads, "tensor", 0, 0, tiled=True)
    half_rows = PROJ // NC
    rows = jnp.sum(grad_parts.astype(F32), axis=0).reshape(pair_count, half_rows, LANES)
    train_rows, query_rows = rows[:train_count], rows[train_count:]
    query_all = lax.all_to_all(
        jnp.broadcast_to(query_rows.astype(BF16), (dp_size, half_rows, LANES)), "dp", 0, 0, tiled=True
    )

    own_curvature = lax.dynamic_index_in_dim(
        curvature.reshape(2, tensor_size // NC, NC, row_share, PROJ), core, 2, keepdims=False
    )
    own_curvature = own_curvature.transpose(1, 2, 0, 3).reshape(half_rows, LANES)
    weighted = own_curvature[None] * train_rows
    self_part = jnp.sum(weighted * train_rows, axis=(1, 2))
    cross_part = jnp.sum(query_all.astype(F32)[:, None] * weighted[None], axis=(2, 3))
    sums = jnp.concatenate([cross_part, self_part[None]], axis=0)
    sums = sums + send(sums, CORE_SWAP)
    scores = sums[:dp_size] / jnp.sqrt(sums[dp_size:] + epsilon)
    train_own = lax.dynamic_slice_in_dim(train_rows, place // NC * row_share, row_share, 1)
    train_block = train_own.reshape(train_count, row_share, 2, PROJ).transpose(0, 2, 1, 3)
    return train_block, scores


def solution(mesh):
    return jax.shard_map(
        shards,
        mesh=mesh,
        in_specs=(
            P("dp", None, None, "tensor"),
            P("dp", None, None, "tensor"),
            P("dp", None, None, "tensor"),
            P("dp", None, None, "tensor"),
            P("tensor", None),
            P(),
            P("tensor", None),
            P("tensor", None),
            P(),
            P("dp", None),
            P("dp"),
            P(),
        ),
        out_specs=(P("dp", None, "tensor", None), P(None, "dp")),
        check_vma=False,
    )
```

```python
import jax
import jax.numpy as jnp
from jax import lax
from jax.experimental import pallas as pl
from jax.experimental.pallas import tpu as pltpu
from jax.sharding import PartitionSpec as P

QUERY_DEV = 1
NX, NY, NC = 4, 2, 2
CHIPS = NX * NY
PROJ = 64
LANES = 128
highest = lax.Precision.HIGHEST
epsilon = 1e-06
F32, BF16 = jnp.float32, jnp.bfloat16
VMEM_LIMIT = 24 * 1024 * 1024


def moves(step):
    pairs = []
    for x in range(NX):
        for y in range(NY):
            for c in range(NC):
                tx, ty, tc = step(x, y, c)
                source = (x * NY + y) * NC + c
                target = ((tx % NX) * NY + ty % NY) * NC + tc % NC
                pairs.append((source, target))
    return pairs


X_UP = moves(lambda x, y, c: (x + 1, y, c))
X_DOWN = moves(lambda x, y, c: (x - 1, y, c))
Y_SWAP = moves(lambda x, y, c: (x, y + 1, c))
CORE_SWAP = moves(lambda x, y, c: (x, y, c + 1))
Y_OR_X = moves(lambda x, y, c: (x + c, y + 1 - c, c))

VMEM = pl.BlockSpec(memory_space=pltpu.VMEM)
ANY = pl.BlockSpec(memory_space=pl.ANY)
SMEM = pl.BlockSpec(memory_space=pltpu.SMEM)
PARAMS = pltpu.CompilerParams(vmem_limit_bytes=VMEM_LIMIT)


def send(value, pairs):
    return lax.ppermute(value, "tensor", pairs)


def dot_rows(a, b, precision=None):
    return lax.dot_general(a, b, (((0,), (0,)), ((), ())), precision=precision, preferred_element_type=F32)


def dot_t(a, b):
    return lax.dot_general(a, b, (((1,), (1,)), ((), ())), preferred_element_type=F32)


def in_hbm(array):
    return pltpu.with_memory_space_constraint(array, pltpu.HBM)


def in_vmem(array):
    return pltpu.with_memory_space_constraint(array, pltpu.VMEM)


def first(place, flat, inputs, in_basis_t):
    tokens, width = flat.shape

    def body(place_ref, ref, in_ref, basis_ref, own_ref):
        own_ref[:width, :] = ref[...].T
        own_ref[width:, :] = dot_t(basis_ref[...], in_ref[...]).astype(BF16)

    def whole(shape):
        return pl.BlockSpec(shape, lambda i, place_ref: (0, 0))

    shape = (width + PROJ, tokens)
    return pl.pallas_call(
        body,
        grid_spec=pltpu.PrefetchScalarGridSpec(
            num_scalar_prefetch=1,
            grid=(1,),
            in_specs=[
                whole((tokens, width)),
                whole((tokens, width)),
                pl.BlockSpec((PROJ, width), lambda i, place_ref: (0, place_ref[0])),
            ],
            out_specs=whole(shape),
        ),
        out_shape=jax.ShapeDtypeStruct(shape, BF16),
        compiler_params=PARAMS,
        name="first",
    )(place, in_hbm(flat), in_hbm(inputs), in_hbm(in_basis_t))


def prepare(gate, up_out, down_in_basis_t):
    tokens, hidden = gate.shape
    block = tokens // 2

    def body(gate_ref, up_ref, down_ref, g_ref, act_ref):
        raw = gate_ref[...]
        value = raw.astype(F32)
        value = value / (1.0 + jnp.exp(-value))
        activation = (value * up_ref[...].astype(F32)).astype(BF16)
        act_ref[...] = dot_t(down_ref[...], activation)
        g_ref[...] = raw.T

    return pl.pallas_call(
        body,
        grid=(tokens // block,),
        in_specs=[
            pl.BlockSpec((block, hidden), lambda i: (i, 0)),
            pl.BlockSpec((block, hidden), lambda i: (i, 0)),
            pl.BlockSpec((PROJ, hidden), lambda i: (0, 0)),
        ],
        out_specs=(
            pl.BlockSpec((hidden, block), lambda i: (0, i)),
            pl.BlockSpec((PROJ, block), lambda i: (0, i)),
        ),
        out_shape=(
            pltpu.VMEM((hidden, tokens), BF16),
            pltpu.HBM((PROJ, tokens), F32),
        ),
        compiler_params=PARAMS,
        name="prepare",
    )(in_hbm(gate), in_hbm(up_out), in_hbm(down_in_basis_t))


class Stage:
    chunk = 256
    block = 256

    def __init__(self, count, width, hidden, tokens):
        self.count, self.width, self.hidden, self.tokens = count, width, hidden, tokens
        self.steps, self.blocks = hidden // self.chunk, tokens // self.block
        self.depth = NC * count * width
        self.weights_shape = (PROJ + hidden, self.depth)

    def scratch(self):
        pieces = NC * self.count
        return [
            pltpu.VMEM((self.depth, self.tokens), BF16),
            pltpu.VMEM((pieces * PROJ, self.tokens), BF16),
            pltpu.VMEM((self.hidden, self.tokens), BF16),
            pltpu.SemaphoreType.DMA((self.blocks + 1, pieces)),
        ]

    def feature_copies(self, core, refs, cat, proj, sem):
        groups = [[] for _ in range(self.blocks + 1)]
        width, block = self.width, self.block
        for i, ref in enumerate(refs):
            side = core if i % NC == 0 else 1 - core
            row = pl.multiple_of((i // NC * NC + side) * width, width)
            for t in range(self.blocks):
                span = pl.ds(t * block, block)
                target = cat.at[pl.ds(row, width), span]
                groups[t].append(pltpu.make_async_copy(ref.at[pl.ds(0, width), span], target, sem.at[t, i]))
            target = proj.at[pl.ds(i * PROJ, PROJ)]
            source = ref.at[pl.ds(width, PROJ)]
            groups[-1].append(pltpu.make_async_copy(source, target, sem.at[self.blocks, i]))
        return groups

    def weight_copies(self, chips_ref, first_chip, w_hbm, out_hbm, w_ref, sem):
        wide = NC * self.width
        groups = [[] for _ in range(self.steps)]
        for i in range(self.count):
            source = pl.ds(pl.multiple_of(chips_ref[first_chip + i] * wide, wide), wide)
            target = pl.ds(i * wide, wide)
            groups[0].append(
                pltpu.make_async_copy(
                    out_hbm.at[:, source], w_ref.at[pl.ds(0, PROJ), target], sem.at[self.steps, i]
                )
            )
            for step in range(self.steps):
                rows = pl.ds(step * self.chunk, self.chunk)
                to_rows = pl.ds(PROJ + step * self.chunk, self.chunk)
                groups[step].append(
                    pltpu.make_async_copy(w_hbm.at[rows, source], w_ref.at[to_rows, target], sem.at[step, i])
                )
        return groups

    def weight_semaphores(self):
        return pltpu.SemaphoreType.DMA((self.steps + 1, self.count))

    def span(self, t):
        return slice(t * self.block, (t + 1) * self.block)

    def dots(self, step, t, w_ref, g_ref, cat, scaled):
        h, span = step * self.chunk, self.span(t)
        skip = PROJ if step == 0 else 0
        rows = slice(PROJ + h - skip, PROJ + h + self.chunk)
        grad = jnp.dot(w_ref[rows, :], cat[:, span], preferred_element_type=F32)
        gate = g_ref[h : h + self.chunk, span].astype(F32)
        gate = gate / (1.0 + jnp.exp(-gate))
        scaled[h : h + self.chunk, span] = (grad[skip:] * gate).astype(BF16)
        return grad[:skip]

    def projections(self, proj):
        total = proj[:PROJ, :].astype(F32)
        for i in range(1, NC * self.count):
            total = total + proj[i * PROJ : (i + 1) * PROJ, :].astype(F32)
        return total

    def cost(self):
        return pl.CostEstimate(
            flops=2 * self.tokens * self.hidden * (self.depth + LANES),
            bytes_accessed=2 * self.depth * (self.tokens + self.hidden),
            transcendentals=2 * self.tokens * self.hidden,
        )


def start(copies):
    for copy in copies:
        copy.start()


def wait(copies):
    for copy in copies:
        copy.wait()


def middle_stage(core, chips, first_chip, pieces, weights, gates, basis_t, out_basis_t, before=None):
    count = len(pieces) // NC
    height, tokens = pieces[0].shape
    hidden = gates.shape[0]
    plan = Stage(count, height - PROJ, hidden, tokens)

    def body(core_ref, chips_ref, *refs):
        refs = list(refs)
        piece_refs = [refs.pop(0) for _ in pieces]
        w_hbm, out_hbm, g_ref, b_ref = [refs.pop(0) for _ in range(4)]
        before_ref = refs.pop(0) if before is not None else None
        sums = refs.pop(0)
        cat, proj, scaled, sem, w_ref, w_sem = refs[:6]
        features = plan.feature_copies(core_ref[0], piece_refs, cat, proj, sem)
        columns = plan.weight_copies(chips_ref, first_chip, w_hbm, out_hbm, w_ref, w_sem)
        groups = [(features[i] if i < plan.blocks else []) + columns[i] for i in range(plan.steps)]
        start(groups[0])
        start(groups[1])
        for i in range(plan.steps):
            wait(groups[i])
            if i + 2 < plan.steps:
                start(groups[i + 2])
            elif i + 2 == plan.steps:
                start(features[-1])
            for step in range(i + 1):
                for t in range(min(i + 1, plan.blocks)):
                    if step == i or t == i:
                        down = plan.dots(step, t, w_ref, g_ref, cat, scaled)
                        if step == 0:
                            rows = slice(PROJ, 2 * PROJ)
                            if before_ref is not None:
                                down = down + before_ref[rows, plan.span(t)]
                            sums[rows, plan.span(t)] = down
        for t in range(plan.blocks):
            span = plan.span(t)
            up = jnp.dot(b_ref[...], scaled[:, span], preferred_element_type=F32)
            if before_ref is not None:
                up = up + before_ref[:PROJ, span]
            sums[:PROJ, span] = up
        wait(features[-1])
        total = plan.projections(proj)
        if before_ref is not None:
            total = total + before_ref[2 * PROJ :, :]
        sums[2 * PROJ :, :] = total

    operands = [core, chips, *pieces, in_hbm(weights), in_hbm(out_basis_t)]
    operands += [in_vmem(gates), basis_t]
    in_specs = [SMEM, SMEM] + [ANY] * (len(pieces) + 2) + [VMEM, VMEM]
    scratch = plan.scratch() + [pltpu.VMEM(plan.weights_shape, BF16), plan.weight_semaphores()]
    if before is not None:
        operands.append(before)
        in_specs.append(VMEM)
    return pl.pallas_call(
        body,
        in_specs=in_specs,
        out_specs=VMEM,
        out_shape=jax.ShapeDtypeStruct((3 * PROJ, tokens), F32),
        scratch_shapes=scratch,
        compiler_params=PARAMS,
        cost_estimate=plan.cost(),
        name="middle_stage",
    )(*operands)


def last_stage(
    core, chips, first_chip, lengths, pair_weights, pieces, before, weights, gates, basis_t, out_basis_t, act, seq_len, devices
):
    count = len(pieces) // NC
    height, tokens = pieces[0].shape
    hidden = gates.shape[0]
    plan = Stage(count, height - PROJ, hidden, tokens)
    pair_tokens = 2 * seq_len
    pairs = tokens // pair_tokens
    share = PROJ // devices

    def body(core_ref, chips_ref, lengths_ref, pair_ref, *refs):
        piece_refs, refs = refs[: len(pieces)], refs[len(pieces) :]
        before_ref, w_hbm, out_hbm, g_ref, b_ref, act_ref, o_ref = refs[:7]
        cat, proj, scaled, sem, left, sums, act_sem, w_ref, w_sem = refs[7:]
        columns = plan.weight_copies(chips_ref, first_chip, w_hbm, out_hbm, w_ref, w_sem)
        features = plan.feature_copies(core_ref[0], piece_refs, cat, proj, sem)
        act_copy = pltpu.make_async_copy(act_ref, left.at[pl.ds(PROJ, PROJ)], act_sem)
        start(features[0])
        for group in columns:
            start(group)
        start(features[1] + [act_copy])
        for t in range(plan.blocks):
            wait(features[t])
            if t + 2 <= plan.blocks:
                start(features[t + 2])
            span = plan.span(t)
            for step in range(plan.steps):
                if t == 0:
                    wait(columns[step])
                down = plan.dots(step, t, w_ref, g_ref, cat, scaled)
                if step == 0:
                    sums[PROJ:, span] = down + before_ref[PROJ : 2 * PROJ, span]
            up = jnp.dot(b_ref[...], scaled[:, span], preferred_element_type=F32)
            sums[:PROJ, span] = up + before_ref[:PROJ, span]
        wait(features[-1] + [act_copy])
        left[:PROJ, :] = plan.projections(proj) + before_ref[2 * PROJ :, :]
        lane = lax.broadcasted_iota(jnp.int32, (1, seq_len), 1)
        for s in range(tokens // seq_len):
            columns = slice(s * seq_len, (s + 1) * seq_len)
            sign = 1.0 if s % 2 == 0 else -1.0
            factor = jnp.where(lane < lengths_ref[s // 2, s % 2], pair_ref[s // 2] * sign, 0.0)
            left[:, columns] = left[:, columns] * factor
        half = lax.broadcasted_iota(jnp.int32, (PROJ, LANES), 1) < PROJ
        for pair in range(pairs):
            span = slice(pair * pair_tokens, (pair + 1) * pair_tokens)
            a, b = left[:, span], sums[:, span]
            a_high, b_high = a.astype(BF16), b.astype(BF16)
            a_low, b_low = (a - a_high.astype(F32)).astype(BF16), (b - b_high.astype(F32)).astype(BF16)
            both = dot_t(
                jnp.concatenate([a_high, a_high, a_low], axis=1), jnp.concatenate([b_high, b_low, b_high], axis=1)
            )
            grads = jnp.where(half, both[:PROJ], both[PROJ:])
            for c in range(NC):
                blocks = [grads[k * share : (k + 1) * share] for k in range(c, devices, NC)]
                mine = jnp.concatenate(blocks, axis=0).astype(BF16)
                for k in range(c, devices, NC):
                    o_ref[k, pair * PROJ // NC : (pair + 1) * PROJ // NC, :] = mine

    return pl.pallas_call(
        body,
        in_specs=[SMEM] * 4 + [ANY] * len(pieces) + [VMEM, ANY, ANY, VMEM, VMEM, ANY],
        out_specs=VMEM,
        out_shape=jax.ShapeDtypeStruct((devices, pairs * PROJ // NC, LANES), BF16),
        scratch_shapes=plan.scratch()
        + [pltpu.VMEM((2 * PROJ, tokens), F32), pltpu.VMEM((2 * PROJ, tokens), F32), pltpu.SemaphoreType.DMA]
        + [pltpu.VMEM(plan.weights_shape, BF16), plan.weight_semaphores()],
        compiler_params=PARAMS,
        cost_estimate=plan.cost(),
        name="last_stage",
    )(
        core, chips, lengths, pair_weights, *pieces,
        before, in_hbm(weights), in_hbm(out_basis_t), in_vmem(gates), basis_t, in_hbm(act),
    )


def shards(
    inputs,
    cotangent,
    gate_pre,
    up_out,
    w_down,
    up_in_basis,
    up_out_basis,
    down_in_basis,
    down_out_basis,
    lengths,
    margins,
    curvature,
):
    pair_count = inputs.shape[0]
    seq_len = inputs.shape[2]
    width = inputs.shape[3]
    hidden = gate_pre.shape[3]
    token_count = pair_count * 2 * seq_len
    train_count = pair_count - QUERY_DEV
    dp_size = lax.axis_size("dp")
    tensor_size = lax.axis_size("tensor")
    row_share = PROJ // tensor_size
    place = lax.axis_index("tensor")
    x, y, core = place // (NY * NC), (place // NC) % NY, place % NC

    own = first(
        place[None],
        cotangent.reshape(token_count, width),
        inputs.reshape(token_count, width),
        up_in_basis.T,
    )
    gates, act = prepare(
        gate_pre.reshape(token_count, hidden),
        up_out.reshape(token_count, hidden),
        down_in_basis.T,
    )
    pair_weights = 1.0 / (1.0 + jnp.exp(margins))

    def chip_at(dx, row):
        return ((x + dx) % NX) * NY + row

    flip = 1 - y
    near_chips = [chip_at(0, y), chip_at(3, y), chip_at(1, y), chip_at(0, flip)]
    far_chips = [chip_at(2, y), chip_at(1, flip), chip_at(3, flip), chip_at(2, flip)]
    chips = jnp.stack(near_chips + far_chips).astype(jnp.int32)
    bases = (up_out_basis.T, down_out_basis.T)

    def with_twins(pieces):
        return [shard for piece in pieces for shard in (piece, send(piece, CORE_SWAP))]

    near = (send(own, X_UP), send(own, X_DOWN), send(own, Y_SWAP))
    sums = middle_stage(core[None], chips, 0, with_twins([own]), w_down, gates, *bases)
    left_own, first_sums = lax.optimization_barrier((near[0], sums))
    right_own, across, sums = lax.optimization_barrier((*near[1:], first_sums))
    near = (left_own, right_own, across)
    x2, pr, pl_ = send(left_own, X_UP), send(across, X_DOWN), send(left_own, Y_SWAP)
    sums = middle_stage(core[None], chips, 1, with_twins(near), w_down, gates, *bases, before=sums)
    third, far, sums = lax.optimization_barrier((jnp.where(core == 0, x2, pl_), (x2, pr, pl_), sums))
    last_hop = send(third, Y_OR_X)
    sums = middle_stage(core[None], chips, 4, with_twins(far), w_down, gates, *bases, before=sums)
    last_hop, sums = lax.optimization_barrier((last_hop, sums))
    grads = last_stage(
        core[None], chips, 7, lengths, pair_weights, with_twins([last_hop]),
        sums, w_down, gates, *bases, act, seq_len, tensor_size,
    )
    grad_parts = lax.all_to_all(grads, "tensor", 0, 0, tiled=True)
    half_rows = PROJ // NC
    rows = jnp.sum(grad_parts.astype(F32), axis=0).reshape(pair_count, half_rows, LANES)
    train_rows, query_rows = rows[:train_count], rows[train_count:]
    query_all = lax.all_to_all(
        jnp.broadcast_to(query_rows.astype(BF16), (dp_size, half_rows, LANES)), "dp", 0, 0, tiled=True
    )

    own_curvature = lax.dynamic_index_in_dim(
        curvature.reshape(2, tensor_size // NC, NC, row_share, PROJ), core, 2, keepdims=False
    )
    own_curvature = own_curvature.transpose(1, 2, 0, 3).reshape(half_rows, LANES)
    weighted = own_curvature[None] * train_rows
    self_part = jnp.sum(weighted * train_rows, axis=(1, 2))
    cross_part = jnp.sum(query_all.astype(F32)[:, None] * weighted[None], axis=(2, 3))
    sums = jnp.concatenate([cross_part, self_part[None]], axis=0)
    sums = sums + send(sums, CORE_SWAP)
    scores = sums[:dp_size] / jnp.sqrt(sums[dp_size:] + epsilon)
    train_own = lax.dynamic_slice_in_dim(train_rows, place // NC * row_share, row_share, 1)
    train_block = train_own.reshape(train_count, row_share, 2, PROJ).transpose(0, 2, 1, 3)
    return train_block, scores


def solution(mesh):
    return jax.shard_map(
        shards,
        mesh=mesh,
        in_specs=(
            P("dp", None, None, "tensor"),
            P("dp", None, None, "tensor"),
            P("dp", None, None, "tensor"),
            P("dp", None, None, "tensor"),
            P("tensor", None),
            P(),
            P("tensor", None),
            P("tensor", None),
            P(),
            P("dp", None),
            P("dp"),
            P(),
        ),
        out_specs=(P("dp", None, "tensor", None), P(None, "dp")),
        check_vma=False,
    )
```

```python
import jax
import jax.numpy as jnp
from jax import lax
from jax.experimental import pallas as pl
from jax.experimental.pallas import tpu as pltpu
from jax.sharding import PartitionSpec as P

QUERY_DEV = 1
NX, NY, NC = 4, 2, 2
CHIPS = NX * NY
PROJ = 64
LANES = 128
highest = lax.Precision.HIGHEST
epsilon = 1e-06
F32, BF16 = jnp.float32, jnp.bfloat16
VMEM_LIMIT = 24 * 1024 * 1024


def moves(step):
    pairs = []
    for x in range(NX):
        for y in range(NY):
            for c in range(NC):
                tx, ty, tc = step(x, y, c)
                source = (x * NY + y) * NC + c
                target = ((tx % NX) * NY + ty % NY) * NC + tc % NC
                pairs.append((source, target))
    return pairs


X_UP = moves(lambda x, y, c: (x + 1, y, c))
X_DOWN = moves(lambda x, y, c: (x - 1, y, c))
Y_SWAP = moves(lambda x, y, c: (x, y + 1, c))
CORE_SWAP = moves(lambda x, y, c: (x, y, c + 1))
X_OR_Y = moves(lambda x, y, c: (x + 1 - c, y + c, c))
Y_OR_X = moves(lambda x, y, c: (x + c, y + 1 - c, c))

VMEM = pl.BlockSpec(memory_space=pltpu.VMEM)
ANY = pl.BlockSpec(memory_space=pl.ANY)
SMEM = pl.BlockSpec(memory_space=pltpu.SMEM)
PARAMS = pltpu.CompilerParams(vmem_limit_bytes=VMEM_LIMIT)


def send(value, pairs):
    return lax.ppermute(value, "tensor", pairs)


def dot_rows(a, b, precision=None):
    return lax.dot_general(a, b, (((0,), (0,)), ((), ())), precision=precision, preferred_element_type=F32)


def dot_t(a, b):
    return lax.dot_general(a, b, (((1,), (1,)), ((), ())), preferred_element_type=F32)


def in_hbm(array):
    return pltpu.with_memory_space_constraint(array, pltpu.HBM)


def in_vmem(array):
    return pltpu.with_memory_space_constraint(array, pltpu.VMEM)


def first(place, flat, inputs, in_basis_t):
    tokens, width = flat.shape

    def body(place_ref, ref, in_ref, basis_ref, own_ref):
        own_ref[:width, :] = ref[...].T
        own_ref[width:, :] = dot_t(basis_ref[...], in_ref[...]).astype(BF16)

    def whole(shape):
        return pl.BlockSpec(shape, lambda i, place_ref: (0, 0))

    shape = (width + PROJ, tokens)
    return pl.pallas_call(
        body,
        grid_spec=pltpu.PrefetchScalarGridSpec(
            num_scalar_prefetch=1,
            grid=(1,),
            in_specs=[
                whole((tokens, width)),
                whole((tokens, width)),
                pl.BlockSpec((PROJ, width), lambda i, place_ref: (0, place_ref[0])),
            ],
            out_specs=whole(shape),
        ),
        out_shape=jax.ShapeDtypeStruct(shape, BF16),
        compiler_params=PARAMS,
        name="first",
    )(place, in_hbm(flat), in_hbm(inputs), in_hbm(in_basis_t))


def prepare(gate, up_out, down_in_basis_t):
    tokens, hidden = gate.shape
    block = tokens // 2

    def body(gate_ref, up_ref, down_ref, g_ref, act_ref):
        raw = gate_ref[...]
        value = raw.astype(F32)
        value = value / (1.0 + jnp.exp(-value))
        activation = (value * up_ref[...].astype(F32)).astype(BF16)
        act_ref[...] = dot_t(down_ref[...], activation)
        g_ref[...] = raw.T

    return pl.pallas_call(
        body,
        grid=(tokens // block,),
        in_specs=[
            pl.BlockSpec((block, hidden), lambda i: (i, 0)),
            pl.BlockSpec((block, hidden), lambda i: (i, 0)),
            pl.BlockSpec((PROJ, hidden), lambda i: (0, 0)),
        ],
        out_specs=(
            pl.BlockSpec((hidden, block), lambda i: (0, i)),
            pl.BlockSpec((PROJ, block), lambda i: (0, i)),
        ),
        out_shape=(
            pltpu.VMEM((hidden, tokens), BF16),
            pltpu.HBM((PROJ, tokens), F32),
        ),
        compiler_params=PARAMS,
        name="prepare",
    )(in_hbm(gate), in_hbm(up_out), in_hbm(down_in_basis_t))


class Stage:
    chunk = 256
    block = 256

    def __init__(self, count, width, hidden, tokens):
        self.count, self.width, self.hidden, self.tokens = count, width, hidden, tokens
        self.steps, self.blocks = hidden // self.chunk, tokens // self.block
        self.depth = NC * count * width
        self.weights_shape = (PROJ + hidden, self.depth)

    def scratch(self):
        pieces = NC * self.count
        return [
            pltpu.VMEM((self.depth, self.tokens), BF16),
            pltpu.VMEM((pieces * PROJ, self.tokens), BF16),
            pltpu.VMEM((self.hidden, self.tokens), BF16),
            pltpu.SemaphoreType.DMA((self.blocks + 1, pieces)),
        ]

    def feature_copies(self, core, refs, cat, proj, sem):
        groups = [[] for _ in range(self.blocks + 1)]
        width, block = self.width, self.block
        for i, ref in enumerate(refs):
            side = core if i % NC == 0 else 1 - core
            row = pl.multiple_of((i // NC * NC + side) * width, width)
            for t in range(self.blocks):
                span = pl.ds(t * block, block)
                target = cat.at[pl.ds(row, width), span]
                groups[t].append(pltpu.make_async_copy(ref.at[pl.ds(0, width), span], target, sem.at[t, i]))
            target = proj.at[pl.ds(i * PROJ, PROJ)]
            source = ref.at[pl.ds(width, PROJ)]
            groups[-1].append(pltpu.make_async_copy(source, target, sem.at[self.blocks, i]))
        return groups

    def weight_copies(self, chips_ref, first_chip, w_hbm, out_hbm, w_ref, sem):
        wide = NC * self.width
        groups = [[] for _ in range(self.steps)]
        for i in range(self.count):
            source = pl.ds(pl.multiple_of(chips_ref[first_chip + i] * wide, wide), wide)
            target = pl.ds(i * wide, wide)
            groups[0].append(
                pltpu.make_async_copy(
                    out_hbm.at[:, source], w_ref.at[pl.ds(0, PROJ), target], sem.at[self.steps, i]
                )
            )
            for step in range(self.steps):
                rows = pl.ds(step * self.chunk, self.chunk)
                to_rows = pl.ds(PROJ + step * self.chunk, self.chunk)
                groups[step].append(
                    pltpu.make_async_copy(w_hbm.at[rows, source], w_ref.at[to_rows, target], sem.at[step, i])
                )
        return groups

    def weight_semaphores(self):
        return pltpu.SemaphoreType.DMA((self.steps + 1, self.count))

    def span(self, t):
        return slice(t * self.block, (t + 1) * self.block)

    def dots(self, step, t, w_ref, g_ref, cat, scaled):
        h, span = step * self.chunk, self.span(t)
        skip = PROJ if step == 0 else 0
        rows = slice(PROJ + h - skip, PROJ + h + self.chunk)
        grad = jnp.dot(w_ref[rows, :], cat[:, span], preferred_element_type=F32)
        gate = g_ref[h : h + self.chunk, span].astype(F32)
        gate = gate / (1.0 + jnp.exp(-gate))
        scaled[h : h + self.chunk, span] = (grad[skip:] * gate).astype(BF16)
        return grad[:skip]

    def projections(self, proj):
        total = proj[:PROJ, :].astype(F32)
        for i in range(1, NC * self.count):
            total = total + proj[i * PROJ : (i + 1) * PROJ, :].astype(F32)
        return total

    def cost(self):
        return pl.CostEstimate(
            flops=2 * self.tokens * self.hidden * (self.depth + LANES),
            bytes_accessed=2 * self.depth * (self.tokens + self.hidden),
            transcendentals=2 * self.tokens * self.hidden,
        )


def start(copies):
    for copy in copies:
        copy.start()


def wait(copies):
    for copy in copies:
        copy.wait()


def middle_stage(core, chips, first_chip, pieces, weights, gates, basis_t, out_basis_t, before=None):
    count = len(pieces) // NC
    height, tokens = pieces[0].shape
    hidden = gates.shape[0]
    plan = Stage(count, height - PROJ, hidden, tokens)

    def body(core_ref, chips_ref, *refs):
        refs = list(refs)
        piece_refs = [refs.pop(0) for _ in pieces]
        w_hbm, out_hbm, g_ref, b_ref = [refs.pop(0) for _ in range(4)]
        before_ref = refs.pop(0) if before is not None else None
        sums = refs.pop(0)
        cat, proj, scaled, sem, w_ref, w_sem = refs[:6]
        features = plan.feature_copies(core_ref[0], piece_refs, cat, proj, sem)
        columns = plan.weight_copies(chips_ref, first_chip, w_hbm, out_hbm, w_ref, w_sem)
        groups = [(features[i] if i < plan.blocks else []) + columns[i] for i in range(plan.steps)]
        start(groups[0])
        start(groups[1])
        for i in range(plan.steps):
            wait(groups[i])
            if i + 2 < plan.steps:
                start(groups[i + 2])
            elif i + 2 == plan.steps:
                start(features[-1])
            for step in range(i + 1):
                for t in range(min(i + 1, plan.blocks)):
                    if step == i or t == i:
                        down = plan.dots(step, t, w_ref, g_ref, cat, scaled)
                        if step == 0:
                            rows = slice(PROJ, 2 * PROJ)
                            if before_ref is not None:
                                down = down + before_ref[rows, plan.span(t)]
                            sums[rows, plan.span(t)] = down
        for t in range(plan.blocks):
            span = plan.span(t)
            up = jnp.dot(b_ref[...], scaled[:, span], preferred_element_type=F32)
            if before_ref is not None:
                up = up + before_ref[:PROJ, span]
            sums[:PROJ, span] = up
        wait(features[-1])
        total = plan.projections(proj)
        if before_ref is not None:
            total = total + before_ref[2 * PROJ :, :]
        sums[2 * PROJ :, :] = total

    operands = [core, chips, *pieces, in_hbm(weights), in_hbm(out_basis_t)]
    operands += [in_vmem(gates), basis_t]
    in_specs = [SMEM, SMEM] + [ANY] * (len(pieces) + 2) + [VMEM, VMEM]
    scratch = plan.scratch() + [pltpu.VMEM(plan.weights_shape, BF16), plan.weight_semaphores()]
    if before is not None:
        operands.append(before)
        in_specs.append(VMEM)
    return pl.pallas_call(
        body,
        in_specs=in_specs,
        out_specs=VMEM,
        out_shape=jax.ShapeDtypeStruct((3 * PROJ, tokens), F32),
        scratch_shapes=scratch,
        compiler_params=PARAMS,
        cost_estimate=plan.cost(),
        name="middle_stage",
    )(*operands)


def last_stage(
    core, chips, first_chip, lengths, pair_weights, pieces, before, weights, gates, basis_t, out_basis_t, act, seq_len, devices
):
    count = len(pieces) // NC
    height, tokens = pieces[0].shape
    hidden = gates.shape[0]
    plan = Stage(count, height - PROJ, hidden, tokens)
    pair_tokens = 2 * seq_len
    pairs = tokens // pair_tokens
    share = PROJ // devices

    def body(core_ref, chips_ref, lengths_ref, pair_ref, *refs):
        piece_refs, refs = refs[: len(pieces)], refs[len(pieces) :]
        before_ref, w_hbm, out_hbm, g_ref, b_ref, act_ref, o_ref = refs[:7]
        cat, proj, scaled, sem, left, sums, act_sem, w_ref, w_sem = refs[7:]
        columns = plan.weight_copies(chips_ref, first_chip, w_hbm, out_hbm, w_ref, w_sem)
        features = plan.feature_copies(core_ref[0], piece_refs, cat, proj, sem)
        act_copy = pltpu.make_async_copy(act_ref, left.at[pl.ds(PROJ, PROJ)], act_sem)
        start(features[0])
        for group in columns:
            start(group)
        start(features[1] + [act_copy])
        for t in range(plan.blocks):
            wait(features[t])
            if t + 2 <= plan.blocks:
                start(features[t + 2])
            span = plan.span(t)
            for step in range(plan.steps):
                if t == 0:
                    wait(columns[step])
                down = plan.dots(step, t, w_ref, g_ref, cat, scaled)
                if step == 0:
                    sums[PROJ:, span] = down + before_ref[PROJ : 2 * PROJ, span]
            up = jnp.dot(b_ref[...], scaled[:, span], preferred_element_type=F32)
            sums[:PROJ, span] = up + before_ref[:PROJ, span]
        wait(features[-1] + [act_copy])
        left[:PROJ, :] = plan.projections(proj) + before_ref[2 * PROJ :, :]
        lane = lax.broadcasted_iota(jnp.int32, (1, seq_len), 1)
        for s in range(tokens // seq_len):
            columns = slice(s * seq_len, (s + 1) * seq_len)
            sign = 1.0 if s % 2 == 0 else -1.0
            factor = jnp.where(lane < lengths_ref[s // 2, s % 2], pair_ref[s // 2] * sign, 0.0)
            left[:, columns] = left[:, columns] * factor
        half = lax.broadcasted_iota(jnp.int32, (PROJ, LANES), 1) < PROJ
        for pair in range(pairs):
            span = slice(pair * pair_tokens, (pair + 1) * pair_tokens)
            a, b = left[:, span], sums[:, span]
            a_high, b_high = a.astype(BF16), b.astype(BF16)
            a_low, b_low = (a - a_high.astype(F32)).astype(BF16), (b - b_high.astype(F32)).astype(BF16)
            both = dot_t(
                jnp.concatenate([a_high, a_high, a_low], axis=1), jnp.concatenate([b_high, b_low, b_high], axis=1)
            )
            grads = jnp.where(half, both[:PROJ], both[PROJ:])
            for c in range(NC):
                blocks = [grads[k * share : (k + 1) * share] for k in range(c, devices, NC)]
                mine = jnp.concatenate(blocks, axis=0).astype(BF16)
                for k in range(c, devices, NC):
                    o_ref[k, pair * PROJ // NC : (pair + 1) * PROJ // NC, :] = mine

    return pl.pallas_call(
        body,
        in_specs=[SMEM] * 4 + [ANY] * len(pieces) + [VMEM, ANY, ANY, VMEM, VMEM, ANY],
        out_specs=VMEM,
        out_shape=jax.ShapeDtypeStruct((devices, pairs * PROJ // NC, LANES), BF16),
        scratch_shapes=plan.scratch()
        + [pltpu.VMEM((2 * PROJ, tokens), F32), pltpu.VMEM((2 * PROJ, tokens), F32), pltpu.SemaphoreType.DMA]
        + [pltpu.VMEM(plan.weights_shape, BF16), plan.weight_semaphores()],
        compiler_params=PARAMS,
        cost_estimate=plan.cost(),
        name="last_stage",
    )(
        core, chips, lengths, pair_weights, *pieces,
        before, in_hbm(weights), in_hbm(out_basis_t), in_vmem(gates), basis_t, in_hbm(act),
    )


def shards(
    inputs,
    cotangent,
    gate_pre,
    up_out,
    w_down,
    up_in_basis,
    up_out_basis,
    down_in_basis,
    down_out_basis,
    lengths,
    margins,
    curvature,
):
    pair_count = inputs.shape[0]
    seq_len = inputs.shape[2]
    width = inputs.shape[3]
    hidden = gate_pre.shape[3]
    token_count = pair_count * 2 * seq_len
    train_count = pair_count - QUERY_DEV
    dp_size = lax.axis_size("dp")
    tensor_size = lax.axis_size("tensor")
    row_share = PROJ // tensor_size
    place = lax.axis_index("tensor")
    x, y, core = place // (NY * NC), (place // NC) % NY, place % NC

    own = first(
        place[None],
        cotangent.reshape(token_count, width),
        inputs.reshape(token_count, width),
        up_in_basis.T,
    )
    gates, act = prepare(
        gate_pre.reshape(token_count, hidden),
        up_out.reshape(token_count, hidden),
        down_in_basis.T,
    )
    pair_weights = 1.0 / (1.0 + jnp.exp(margins))

    def chip_at(dx, row):
        return ((x + dx) % NX) * NY + row

    flip = 1 - y
    near_chips = [chip_at(0, y), chip_at(3, y), chip_at(1, y), chip_at(0, flip)]
    opposite, bend = chip_at(2, y), chip_at(3, flip)
    far_chips = [jnp.where(core == 0, opposite, bend), chip_at(1, flip), jnp.where(core == 0, bend, opposite)]
    far_chips.append(chip_at(2, flip))
    chips = jnp.stack(near_chips + far_chips).astype(jnp.int32)
    bases = (up_out_basis.T, down_out_basis.T)

    def with_twins(pieces):
        return [shard for piece in pieces for shard in (piece, send(piece, CORE_SWAP))]

    near = (send(own, X_UP), send(own, X_DOWN), send(own, Y_SWAP))
    sums = middle_stage(core[None], chips, 0, with_twins([own]), w_down, gates, *bases)
    left_own, first_sums = lax.optimization_barrier((near[0], sums))
    right_own, across, sums = lax.optimization_barrier((*near[1:], first_sums))
    near = (left_own, right_own, across)
    straight, right_across, bent = send(left_own, X_OR_Y), send(across, X_DOWN), send(left_own, Y_OR_X)
    sums = middle_stage(core[None], chips, 1, with_twins(near), w_down, gates, *bases, before=sums)
    far, sums = lax.optimization_barrier(((straight, right_across, bent), sums))
    last_hop = send(far[0], Y_OR_X)
    twins = [send(piece, CORE_SWAP) for piece in far]
    shards = [far[0], twins[2], far[1], twins[1], far[2], twins[0]]
    sums = middle_stage(core[None], chips, 4, shards, w_down, gates, *bases, before=sums)
    last_hop, sums = lax.optimization_barrier((last_hop, sums))
    grads = last_stage(
        core[None], chips, 7, lengths, pair_weights, with_twins([last_hop]),
        sums, w_down, gates, *bases, act, seq_len, tensor_size,
    )
    grad_parts = lax.all_to_all(grads, "tensor", 0, 0, tiled=True)
    half_rows = PROJ // NC
    rows = jnp.sum(grad_parts.astype(F32), axis=0).reshape(pair_count, half_rows, LANES)
    train_rows, query_rows = rows[:train_count], rows[train_count:]
    query_all = lax.all_to_all(
        jnp.broadcast_to(query_rows.astype(BF16), (dp_size, half_rows, LANES)), "dp", 0, 0, tiled=True
    )

    own_curvature = lax.dynamic_index_in_dim(
        curvature.reshape(2, tensor_size // NC, NC, row_share, PROJ), core, 2, keepdims=False
    )
    own_curvature = own_curvature.transpose(1, 2, 0, 3).reshape(half_rows, LANES)
    weighted = own_curvature[None] * train_rows
    self_part = jnp.sum(weighted * train_rows, axis=(1, 2))
    cross_part = jnp.sum(query_all.astype(F32)[:, None] * weighted[None], axis=(2, 3))
    sums = jnp.concatenate([cross_part, self_part[None]], axis=0)
    sums = sums + send(sums, CORE_SWAP)
    scores = sums[:dp_size] / jnp.sqrt(sums[dp_size:] + epsilon)
    train_own = lax.dynamic_slice_in_dim(train_rows, place // NC * row_share, row_share, 1)
    train_block = train_own.reshape(train_count, row_share, 2, PROJ).transpose(0, 2, 1, 3)
    return train_block, scores


def solution(mesh):
    return jax.shard_map(
        shards,
        mesh=mesh,
        in_specs=(
            P("dp", None, None, "tensor"),
            P("dp", None, None, "tensor"),
            P("dp", None, None, "tensor"),
            P("dp", None, None, "tensor"),
            P("tensor", None),
            P(),
            P("tensor", None),
            P("tensor", None),
            P(),
            P("dp", None),
            P("dp"),
            P(),
        ),
        out_specs=(P("dp", None, "tensor", None), P(None, "dp")),
        check_vma=False,
    )
```

```python
import jax
import jax.numpy as jnp
from jax import lax
from jax.experimental import pallas as pl
from jax.experimental.pallas import tpu as pltpu
from jax.sharding import PartitionSpec as P

QUERY_DEV = 1
NX, NY, NC = 4, 2, 2
CHIPS = NX * NY
PROJ = 64
LANES = 128
highest = lax.Precision.HIGHEST
epsilon = 1e-06
F32, BF16 = jnp.float32, jnp.bfloat16
VMEM_LIMIT = 24 * 1024 * 1024


def moves(step):
    pairs = []
    for x in range(NX):
        for y in range(NY):
            for c in range(NC):
                tx, ty, tc = step(x, y, c)
                source = (x * NY + y) * NC + c
                target = ((tx % NX) * NY + ty % NY) * NC + tc % NC
                pairs.append((source, target))
    return pairs


X_UP = moves(lambda x, y, c: (x + 1, y, c))
X_DOWN = moves(lambda x, y, c: (x - 1, y, c))
Y_SWAP = moves(lambda x, y, c: (x, y + 1, c))
CORE_SWAP = moves(lambda x, y, c: (x, y, c + 1))
X_OR_Y = moves(lambda x, y, c: (x + 1 - c, y + c, c))
Y_OR_X = moves(lambda x, y, c: (x + c, y + 1 - c, c))

VMEM = pl.BlockSpec(memory_space=pltpu.VMEM)
ANY = pl.BlockSpec(memory_space=pl.ANY)
SMEM = pl.BlockSpec(memory_space=pltpu.SMEM)
PARAMS = pltpu.CompilerParams(vmem_limit_bytes=VMEM_LIMIT)


def send(value, pairs):
    return lax.ppermute(value, "tensor", pairs)


def dot_rows(a, b, precision=None):
    return lax.dot_general(a, b, (((0,), (0,)), ((), ())), precision=precision, preferred_element_type=F32)


def dot_t(a, b):
    return lax.dot_general(a, b, (((1,), (1,)), ((), ())), preferred_element_type=F32)


def in_hbm(array):
    return pltpu.with_memory_space_constraint(array, pltpu.HBM)


def in_vmem(array):
    return pltpu.with_memory_space_constraint(array, pltpu.VMEM)


def first(place, flat, inputs, in_basis_t):
    tokens, width = flat.shape

    def body(place_ref, ref, in_ref, basis_ref, own_ref):
        own_ref[:width, :] = ref[...].T
        own_ref[width:, :] = dot_t(basis_ref[...], in_ref[...]).astype(BF16)

    def whole(shape):
        return pl.BlockSpec(shape, lambda i, place_ref: (0, 0))

    shape = (width + PROJ, tokens)
    return pl.pallas_call(
        body,
        grid_spec=pltpu.PrefetchScalarGridSpec(
            num_scalar_prefetch=1,
            grid=(1,),
            in_specs=[
                whole((tokens, width)),
                whole((tokens, width)),
                pl.BlockSpec((PROJ, width), lambda i, place_ref: (0, place_ref[0])),
            ],
            out_specs=whole(shape),
        ),
        out_shape=jax.ShapeDtypeStruct(shape, BF16),
        compiler_params=PARAMS,
        name="first",
    )(place, in_hbm(flat), in_hbm(inputs), in_hbm(in_basis_t))


def prepare(gate, up_out, down_in_basis_t):
    tokens, hidden = gate.shape
    block = tokens // 2

    def body(gate_ref, up_ref, down_ref, g_ref, act_ref):
        raw = gate_ref[...]
        value = raw.astype(F32)
        value = value / (1.0 + jnp.exp(-value))
        activation = (value * up_ref[...].astype(F32)).astype(BF16)
        act_ref[...] = dot_t(down_ref[...], activation)
        g_ref[...] = raw.T

    return pl.pallas_call(
        body,
        grid=(tokens // block,),
        in_specs=[
            pl.BlockSpec((block, hidden), lambda i: (i, 0)),
            pl.BlockSpec((block, hidden), lambda i: (i, 0)),
            pl.BlockSpec((PROJ, hidden), lambda i: (0, 0)),
        ],
        out_specs=(
            pl.BlockSpec((hidden, block), lambda i: (0, i)),
            pl.BlockSpec((PROJ, block), lambda i: (0, i)),
        ),
        out_shape=(
            pltpu.VMEM((hidden, tokens), BF16),
            pltpu.HBM((PROJ, tokens), F32),
        ),
        compiler_params=PARAMS,
        name="prepare",
    )(in_hbm(gate), in_hbm(up_out), in_hbm(down_in_basis_t))


class Stage:
    chunk = 256
    block = 256

    def __init__(self, count, width, hidden, tokens):
        self.count, self.width, self.hidden, self.tokens = count, width, hidden, tokens
        self.steps, self.blocks = hidden // self.chunk, tokens // self.block
        self.depth = NC * count * width
        self.weights_shape = (PROJ + hidden, self.depth)

    def scratch(self):
        pieces = NC * self.count
        return [
            pltpu.VMEM((self.depth, self.tokens), BF16),
            pltpu.VMEM((pieces * PROJ, self.tokens), BF16),
            pltpu.VMEM((self.hidden, self.tokens), BF16),
            pltpu.SemaphoreType.DMA((self.blocks + 1, pieces)),
        ]

    def feature_copies(self, core, refs, cat, proj, sem):
        groups = [[] for _ in range(self.blocks + 1)]
        width, block = self.width, self.block
        for i, ref in enumerate(refs):
            side = core if i % NC == 0 else 1 - core
            row = pl.multiple_of((i // NC * NC + side) * width, width)
            for t in range(self.blocks):
                span = pl.ds(t * block, block)
                target = cat.at[pl.ds(row, width), span]
                groups[t].append(pltpu.make_async_copy(ref.at[pl.ds(0, width), span], target, sem.at[t, i]))
            target = proj.at[pl.ds(i * PROJ, PROJ)]
            source = ref.at[pl.ds(width, PROJ)]
            groups[-1].append(pltpu.make_async_copy(source, target, sem.at[self.blocks, i]))
        return groups

    def weight_copies(self, chips_ref, first_chip, w_hbm, out_hbm, w_ref, sem):
        wide = NC * self.width
        groups = [[] for _ in range(self.steps)]
        for i in range(self.count):
            source = pl.ds(pl.multiple_of(chips_ref[first_chip + i] * wide, wide), wide)
            target = pl.ds(i * wide, wide)
            groups[0].append(
                pltpu.make_async_copy(
                    out_hbm.at[:, source], w_ref.at[pl.ds(0, PROJ), target], sem.at[self.steps, i]
                )
            )
            for step in range(self.steps):
                rows = pl.ds(step * self.chunk, self.chunk)
                to_rows = pl.ds(PROJ + step * self.chunk, self.chunk)
                groups[step].append(
                    pltpu.make_async_copy(w_hbm.at[rows, source], w_ref.at[to_rows, target], sem.at[step, i])
                )
        return groups

    def weight_semaphores(self):
        return pltpu.SemaphoreType.DMA((self.steps + 1, self.count))

    def span(self, t):
        return slice(t * self.block, (t + 1) * self.block)

    def dots(self, step, t, w_ref, g_ref, cat, scaled):
        h, span = step * self.chunk, self.span(t)
        skip = PROJ if step == 0 else 0
        rows = slice(PROJ + h - skip, PROJ + h + self.chunk)
        grad = jnp.dot(w_ref[rows, :], cat[:, span], preferred_element_type=F32)
        gate = g_ref[h : h + self.chunk, span].astype(F32)
        gate = gate / (1.0 + jnp.exp(-gate))
        scaled[h : h + self.chunk, span] = (grad[skip:] * gate).astype(BF16)
        return grad[:skip]

    def projections(self, proj):
        total = proj[:PROJ, :].astype(F32)
        for i in range(1, NC * self.count):
            total = total + proj[i * PROJ : (i + 1) * PROJ, :].astype(F32)
        return total

    def cost(self):
        return pl.CostEstimate(
            flops=2 * self.tokens * self.hidden * (self.depth + LANES),
            bytes_accessed=2 * self.depth * (self.tokens + self.hidden),
            transcendentals=2 * self.tokens * self.hidden,
        )


def start(copies):
    for copy in copies:
        copy.start()


def wait(copies):
    for copy in copies:
        copy.wait()


def middle_stage(core, chips, first_chip, pieces, weights, gates, basis_t, out_basis_t, before=None):
    count = len(pieces) // NC
    height, tokens = pieces[0].shape
    hidden = gates.shape[0]
    plan = Stage(count, height - PROJ, hidden, tokens)

    def body(core_ref, chips_ref, *refs):
        refs = list(refs)
        piece_refs = [refs.pop(0) for _ in pieces]
        w_hbm, out_hbm, g_ref, b_ref = [refs.pop(0) for _ in range(4)]
        before_ref = refs.pop(0) if before is not None else None
        sums = refs.pop(0)
        cat, proj, scaled, sem, w_ref, w_sem = refs[:6]
        features = plan.feature_copies(core_ref[0], piece_refs, cat, proj, sem)
        columns = plan.weight_copies(chips_ref, first_chip, w_hbm, out_hbm, w_ref, w_sem)
        groups = [(features[i] if i < plan.blocks else []) + columns[i] for i in range(plan.steps)]
        start(groups[0])
        start(groups[1])
        for i in range(plan.steps):
            wait(groups[i])
            if i + 2 < plan.steps:
                start(groups[i + 2])
            elif i + 2 == plan.steps:
                start(features[-1])
            for step in range(i + 1):
                for t in range(min(i + 1, plan.blocks)):
                    if step == i or t == i:
                        down = plan.dots(step, t, w_ref, g_ref, cat, scaled)
                        if step == 0:
                            rows = slice(PROJ, 2 * PROJ)
                            if before_ref is not None:
                                down = down + before_ref[rows, plan.span(t)]
                            sums[rows, plan.span(t)] = down
        for t in range(plan.blocks):
            span = plan.span(t)
            up = jnp.dot(b_ref[...], scaled[:, span], preferred_element_type=F32)
            if before_ref is not None:
                up = up + before_ref[:PROJ, span]
            sums[:PROJ, span] = up
        wait(features[-1])
        total = plan.projections(proj)
        if before_ref is not None:
            total = total + before_ref[2 * PROJ :, :]
        sums[2 * PROJ :, :] = total

    operands = [core, chips, *pieces, in_hbm(weights), in_hbm(out_basis_t)]
    operands += [in_vmem(gates), basis_t]
    in_specs = [SMEM, SMEM] + [ANY] * (len(pieces) + 2) + [VMEM, VMEM]
    scratch = plan.scratch() + [pltpu.VMEM(plan.weights_shape, BF16), plan.weight_semaphores()]
    if before is not None:
        operands.append(before)
        in_specs.append(VMEM)
    return pl.pallas_call(
        body,
        in_specs=in_specs,
        out_specs=VMEM,
        out_shape=jax.ShapeDtypeStruct((3 * PROJ, tokens), F32),
        scratch_shapes=scratch,
        compiler_params=PARAMS,
        cost_estimate=plan.cost(),
        name="middle_stage",
    )(*operands)


def last_stage(
    core, chips, first_chip, lengths, pair_weights, pieces, before, weights, gates, basis_t, out_basis_t, act, seq_len, devices
):
    count = len(pieces) // NC
    height, tokens = pieces[0].shape
    hidden = gates.shape[0]
    plan = Stage(count, height - PROJ, hidden, tokens)
    pair_tokens = 2 * seq_len
    pairs = tokens // pair_tokens
    share = PROJ // devices

    def body(core_ref, chips_ref, lengths_ref, pair_ref, *refs):
        piece_refs, refs = refs[: len(pieces)], refs[len(pieces) :]
        before_ref, w_hbm, out_hbm, g_ref, b_ref, act_ref, o_ref = refs[:7]
        cat, proj, scaled, sem, left, sums, act_sem, w_ref, w_sem = refs[7:]
        columns = plan.weight_copies(chips_ref, first_chip, w_hbm, out_hbm, w_ref, w_sem)
        features = plan.feature_copies(core_ref[0], piece_refs, cat, proj, sem)
        act_copy = pltpu.make_async_copy(act_ref, left.at[pl.ds(PROJ, PROJ)], act_sem)
        start(features[0])
        for group in columns:
            start(group)
        start(features[1] + [act_copy])
        for t in range(plan.blocks):
            wait(features[t])
            if t + 2 <= plan.blocks:
                start(features[t + 2])
            span = plan.span(t)
            for step in range(plan.steps):
                if t == 0:
                    wait(columns[step])
                down = plan.dots(step, t, w_ref, g_ref, cat, scaled)
                if step == 0:
                    sums[PROJ:, span] = down + before_ref[PROJ : 2 * PROJ, span]
            up = jnp.dot(b_ref[...], scaled[:, span], preferred_element_type=F32)
            sums[:PROJ, span] = up + before_ref[:PROJ, span]
        wait(features[-1] + [act_copy])
        left[:PROJ, :] = plan.projections(proj) + before_ref[2 * PROJ :, :]
        lane = lax.broadcasted_iota(jnp.int32, (1, seq_len), 1)
        for s in range(tokens // seq_len):
            columns = slice(s * seq_len, (s + 1) * seq_len)
            sign = 1.0 if s % 2 == 0 else -1.0
            factor = jnp.where(lane < lengths_ref[s // 2, s % 2], pair_ref[s // 2] * sign, 0.0)
            left[:, columns] = left[:, columns] * factor
        half = lax.broadcasted_iota(jnp.int32, (PROJ, LANES), 1) < PROJ
        for pair in range(pairs):
            span = slice(pair * pair_tokens, (pair + 1) * pair_tokens)
            a, b = left[:, span], sums[:, span]
            a_high, b_high = a.astype(BF16), b.astype(BF16)
            a_low, b_low = (a - a_high.astype(F32)).astype(BF16), (b - b_high.astype(F32)).astype(BF16)
            both = dot_t(
                jnp.concatenate([a_high, a_high, a_low], axis=1), jnp.concatenate([b_high, b_low, b_high], axis=1)
            )
            grads = jnp.where(half, both[:PROJ], both[PROJ:])
            for c in range(NC):
                blocks = [grads[k * share : (k + 1) * share] for k in range(c, devices, NC)]
                mine = jnp.concatenate(blocks, axis=0).astype(BF16)
                for k in range(c, devices, NC):
                    o_ref[k, pair * PROJ // NC : (pair + 1) * PROJ // NC, :] = mine

    return pl.pallas_call(
        body,
        in_specs=[SMEM] * 4 + [ANY] * len(pieces) + [VMEM, ANY, ANY, VMEM, VMEM, ANY],
        out_specs=VMEM,
        out_shape=jax.ShapeDtypeStruct((devices, pairs * PROJ // NC, LANES), BF16),
        scratch_shapes=plan.scratch()
        + [pltpu.VMEM((2 * PROJ, tokens), F32), pltpu.VMEM((2 * PROJ, tokens), F32), pltpu.SemaphoreType.DMA]
        + [pltpu.VMEM(plan.weights_shape, BF16), plan.weight_semaphores()],
        compiler_params=PARAMS,
        cost_estimate=plan.cost(),
        name="last_stage",
    )(
        core, chips, lengths, pair_weights, *pieces,
        before, in_hbm(weights), in_hbm(out_basis_t), in_vmem(gates), basis_t, in_hbm(act),
    )


def shards(
    inputs,
    cotangent,
    gate_pre,
    up_out,
    w_down,
    up_in_basis,
    up_out_basis,
    down_in_basis,
    down_out_basis,
    lengths,
    margins,
    curvature,
):
    pair_count = inputs.shape[0]
    seq_len = inputs.shape[2]
    width = inputs.shape[3]
    hidden = gate_pre.shape[3]
    token_count = pair_count * 2 * seq_len
    train_count = pair_count - QUERY_DEV
    dp_size = lax.axis_size("dp")
    tensor_size = lax.axis_size("tensor")
    row_share = PROJ // tensor_size
    place = lax.axis_index("tensor")
    x, y, core = place // (NY * NC), (place // NC) % NY, place % NC

    own = first(
        place[None],
        cotangent.reshape(token_count, width),
        inputs.reshape(token_count, width),
        up_in_basis.T,
    )
    gates, act = prepare(
        gate_pre.reshape(token_count, hidden),
        up_out.reshape(token_count, hidden),
        down_in_basis.T,
    )
    pair_weights = 1.0 / (1.0 + jnp.exp(margins))

    def chip_at(dx, row):
        return ((x + dx) % NX) * NY + row

    flip = 1 - y
    near_chips = [chip_at(0, y), chip_at(3, y), chip_at(1, y), chip_at(0, flip)]
    opposite, bend = chip_at(2, y), chip_at(3, flip)
    far_chips = [jnp.where(core == 0, opposite, bend), chip_at(1, flip), jnp.where(core == 0, bend, opposite)]
    far_chips.append(chip_at(2, flip))
    chips = jnp.stack(near_chips + far_chips).astype(jnp.int32)
    bases = (up_out_basis.T, down_out_basis.T)

    def with_twins(pieces):
        return [shard for piece in pieces for shard in (piece, send(piece, CORE_SWAP))]

    near = (send(own, X_UP), send(own, X_DOWN), send(own, Y_SWAP))
    sums = middle_stage(core[None], chips, 0, with_twins([own]), w_down, gates, *bases)
    left_own, first_sums = lax.optimization_barrier((near[0], sums))
    right_own, across, sums = lax.optimization_barrier((*near[1:], first_sums))
    near = (left_own, right_own, across)
    straight, right_across, bent = send(left_own, X_OR_Y), send(across, X_DOWN), send(left_own, Y_OR_X)
    sums = middle_stage(core[None], chips, 1, with_twins(near), w_down, gates, *bases, before=sums)
    far = [lax.optimization_barrier((piece, sums))[0] for piece in (straight, right_across, bent)]
    last_hop = send(far[0], Y_OR_X)
    twins = [send(piece, CORE_SWAP) for piece in far]
    shards = [far[0], twins[2], far[1], twins[1], far[2], twins[0]]
    sums = middle_stage(core[None], chips, 4, shards, w_down, gates, *bases, before=sums)
    last_hop, sums = lax.optimization_barrier((last_hop, sums))
    grads = last_stage(
        core[None], chips, 7, lengths, pair_weights, with_twins([last_hop]),
        sums, w_down, gates, *bases, act, seq_len, tensor_size,
    )
    grad_parts = lax.all_to_all(grads, "tensor", 0, 0, tiled=True)
    half_rows = PROJ // NC
    rows = jnp.sum(grad_parts.astype(F32), axis=0).reshape(pair_count, half_rows, LANES)
    train_rows, query_rows = rows[:train_count], rows[train_count:]
    query_all = lax.all_to_all(
        jnp.broadcast_to(query_rows.astype(BF16), (dp_size, half_rows, LANES)), "dp", 0, 0, tiled=True
    )

    own_curvature = lax.dynamic_index_in_dim(
        curvature.reshape(2, tensor_size // NC, NC, row_share, PROJ), core, 2, keepdims=False
    )
    own_curvature = own_curvature.transpose(1, 2, 0, 3).reshape(half_rows, LANES)
    weighted = own_curvature[None] * train_rows
    self_part = jnp.sum(weighted * train_rows, axis=(1, 2))
    cross_part = jnp.sum(query_all.astype(F32)[:, None] * weighted[None], axis=(2, 3))
    sums = jnp.concatenate([cross_part, self_part[None]], axis=0)
    sums = sums + send(sums, CORE_SWAP)
    scores = sums[:dp_size] / jnp.sqrt(sums[dp_size:] + epsilon)
    train_own = lax.dynamic_slice_in_dim(train_rows, place // NC * row_share, row_share, 1)
    train_block = train_own.reshape(train_count, row_share, 2, PROJ).transpose(0, 2, 1, 3)
    return train_block, scores


def solution(mesh):
    return jax.shard_map(
        shards,
        mesh=mesh,
        in_specs=(
            P("dp", None, None, "tensor"),
            P("dp", None, None, "tensor"),
            P("dp", None, None, "tensor"),
            P("dp", None, None, "tensor"),
            P("tensor", None),
            P(),
            P("tensor", None),
            P("tensor", None),
            P(),
            P("dp", None),
            P("dp"),
            P(),
        ),
        out_specs=(P("dp", None, "tensor", None), P(None, "dp")),
        check_vma=False,
    )
```

```python
import jax
import jax.numpy as jnp
from jax import lax
from jax.experimental import pallas as pl
from jax.experimental.pallas import tpu as pltpu
from jax.sharding import PartitionSpec as P

QUERY_DEV = 1
NX, NY, NC = 4, 2, 2
CHIPS = NX * NY
PROJ = 64
LANES = 128
highest = lax.Precision.HIGHEST
epsilon = 1e-06
F32, BF16 = jnp.float32, jnp.bfloat16
VMEM_LIMIT = 24 * 1024 * 1024


def moves(step):
    pairs = []
    for x in range(NX):
        for y in range(NY):
            for c in range(NC):
                tx, ty, tc = step(x, y, c)
                source = (x * NY + y) * NC + c
                target = ((tx % NX) * NY + ty % NY) * NC + tc % NC
                pairs.append((source, target))
    return pairs


X_UP = moves(lambda x, y, c: (x + 1, y, c))
X_DOWN = moves(lambda x, y, c: (x - 1, y, c))
Y_SWAP = moves(lambda x, y, c: (x, y + 1, c))
CORE_SWAP = moves(lambda x, y, c: (x, y, c + 1))
X_OR_Y = moves(lambda x, y, c: (x + 1 - c, y + c, c))
Y_OR_X = moves(lambda x, y, c: (x + c, y + 1 - c, c))

VMEM = pl.BlockSpec(memory_space=pltpu.VMEM)
ANY = pl.BlockSpec(memory_space=pl.ANY)
SMEM = pl.BlockSpec(memory_space=pltpu.SMEM)
PARAMS = pltpu.CompilerParams(vmem_limit_bytes=VMEM_LIMIT)


def send(value, pairs):
    return lax.ppermute(value, "tensor", pairs)


def dot_rows(a, b, precision=None):
    return lax.dot_general(a, b, (((0,), (0,)), ((), ())), precision=precision, preferred_element_type=F32)


def dot_t(a, b):
    return lax.dot_general(a, b, (((1,), (1,)), ((), ())), preferred_element_type=F32)


def in_hbm(array):
    return pltpu.with_memory_space_constraint(array, pltpu.HBM)


def in_vmem(array):
    return pltpu.with_memory_space_constraint(array, pltpu.VMEM)


def first(place, flat, inputs, in_basis_t):
    tokens, width = flat.shape

    def body(place_ref, ref, in_ref, basis_ref, own_ref):
        own_ref[:width, :] = ref[...].T
        own_ref[width:, :] = dot_t(basis_ref[...], in_ref[...]).astype(BF16)

    def whole(shape):
        return pl.BlockSpec(shape, lambda i, place_ref: (0, 0))

    shape = (width + PROJ, tokens)
    return pl.pallas_call(
        body,
        grid_spec=pltpu.PrefetchScalarGridSpec(
            num_scalar_prefetch=1,
            grid=(1,),
            in_specs=[
                whole((tokens, width)),
                whole((tokens, width)),
                pl.BlockSpec((PROJ, width), lambda i, place_ref: (0, place_ref[0])),
            ],
            out_specs=whole(shape),
        ),
        out_shape=jax.ShapeDtypeStruct(shape, BF16),
        compiler_params=PARAMS,
        name="first",
    )(place, in_hbm(flat), in_hbm(inputs), in_hbm(in_basis_t))


def prepare(gate, up_out, down_in_basis_t):
    tokens, hidden = gate.shape
    block = tokens // 2

    def body(gate_ref, up_ref, down_ref, g_ref, act_ref):
        raw = gate_ref[...]
        value = raw.astype(F32)
        value = value / (1.0 + jnp.exp(-value))
        activation = (value * up_ref[...].astype(F32)).astype(BF16)
        act_ref[...] = dot_t(down_ref[...], activation)
        g_ref[...] = raw.T

    return pl.pallas_call(
        body,
        grid=(tokens // block,),
        in_specs=[
            pl.BlockSpec((block, hidden), lambda i: (i, 0)),
            pl.BlockSpec((block, hidden), lambda i: (i, 0)),
            pl.BlockSpec((PROJ, hidden), lambda i: (0, 0)),
        ],
        out_specs=(
            pl.BlockSpec((hidden, block), lambda i: (0, i)),
            pl.BlockSpec((PROJ, block), lambda i: (0, i)),
        ),
        out_shape=(
            pltpu.VMEM((hidden, tokens), BF16),
            pltpu.HBM((PROJ, tokens), F32),
        ),
        compiler_params=PARAMS,
        name="prepare",
    )(in_hbm(gate), in_hbm(up_out), in_hbm(down_in_basis_t))


class Stage:
    chunk = 256
    block = 256

    def __init__(self, count, width, hidden, tokens):
        self.count, self.width, self.hidden, self.tokens = count, width, hidden, tokens
        self.steps, self.blocks = hidden // self.chunk, tokens // self.block
        self.depth = NC * count * width
        self.weights_shape = (PROJ + hidden, self.depth)

    def scratch(self):
        pieces = NC * self.count
        return [
            pltpu.VMEM((self.depth, self.tokens), BF16),
            pltpu.VMEM((pieces * PROJ, self.tokens), BF16),
            pltpu.VMEM((self.hidden, self.tokens), BF16),
            pltpu.SemaphoreType.DMA((self.blocks + 1, pieces)),
        ]

    def feature_copies(self, core, refs, cat, proj, sem):
        groups = [[] for _ in range(self.blocks + 1)]
        width, block = self.width, self.block
        for i, ref in enumerate(refs):
            side = core if i % NC == 0 else 1 - core
            row = pl.multiple_of((i // NC * NC + side) * width, width)
            for t in range(self.blocks):
                span = pl.ds(t * block, block)
                target = cat.at[pl.ds(row, width), span]
                groups[t].append(pltpu.make_async_copy(ref.at[pl.ds(0, width), span], target, sem.at[t, i]))
            target = proj.at[pl.ds(i * PROJ, PROJ)]
            source = ref.at[pl.ds(width, PROJ)]
            groups[-1].append(pltpu.make_async_copy(source, target, sem.at[self.blocks, i]))
        return groups

    def weight_copies(self, chips_ref, first_chip, w_hbm, out_hbm, w_ref, sem):
        wide = NC * self.width
        groups = [[] for _ in range(self.steps)]
        for i in range(self.count):
            source = pl.ds(pl.multiple_of(chips_ref[first_chip + i] * wide, wide), wide)
            target = pl.ds(i * wide, wide)
            groups[0].append(
                pltpu.make_async_copy(
                    out_hbm.at[:, source], w_ref.at[pl.ds(0, PROJ), target], sem.at[self.steps, i]
                )
            )
            for step in range(self.steps):
                rows = pl.ds(step * self.chunk, self.chunk)
                to_rows = pl.ds(PROJ + step * self.chunk, self.chunk)
                groups[step].append(
                    pltpu.make_async_copy(w_hbm.at[rows, source], w_ref.at[to_rows, target], sem.at[step, i])
                )
        return groups

    def weight_semaphores(self):
        return pltpu.SemaphoreType.DMA((self.steps + 1, self.count))

    def span(self, t):
        return slice(t * self.block, (t + 1) * self.block)

    def dots(self, step, t, w_ref, g_ref, cat, scaled):
        h, span = step * self.chunk, self.span(t)
        skip = PROJ if step == 0 else 0
        rows = slice(PROJ + h - skip, PROJ + h + self.chunk)
        grad = jnp.dot(w_ref[rows, :], cat[:, span], preferred_element_type=F32)
        gate = g_ref[h : h + self.chunk, span].astype(F32)
        gate = gate / (1.0 + jnp.exp(-gate))
        scaled[h : h + self.chunk, span] = (grad[skip:] * gate).astype(BF16)
        return grad[:skip]

    def projections(self, proj):
        total = proj[:PROJ, :].astype(F32)
        for i in range(1, NC * self.count):
            total = total + proj[i * PROJ : (i + 1) * PROJ, :].astype(F32)
        return total

    def cost(self):
        return pl.CostEstimate(
            flops=2 * self.tokens * self.hidden * (self.depth + LANES),
            bytes_accessed=2 * self.depth * (self.tokens + self.hidden),
            transcendentals=2 * self.tokens * self.hidden,
        )


def start(copies):
    for copy in copies:
        copy.start()


def wait(copies):
    for copy in copies:
        copy.wait()


def middle_stage(core, chips, first_chip, pieces, weights, gates, basis_t, out_basis_t, before=None):
    count = len(pieces) // NC
    height, tokens = pieces[0].shape
    hidden = gates.shape[0]
    plan = Stage(count, height - PROJ, hidden, tokens)

    def body(core_ref, chips_ref, *refs):
        refs = list(refs)
        piece_refs = [refs.pop(0) for _ in pieces]
        w_hbm, out_hbm, g_ref, b_ref = [refs.pop(0) for _ in range(4)]
        before_ref = refs.pop(0) if before is not None else None
        sums = refs.pop(0)
        cat, proj, scaled, sem, w_ref, w_sem = refs[:6]
        features = plan.feature_copies(core_ref[0], piece_refs, cat, proj, sem)
        columns = plan.weight_copies(chips_ref, first_chip, w_hbm, out_hbm, w_ref, w_sem)
        groups = [(features[i] if i < plan.blocks else []) + columns[i] for i in range(plan.steps)]
        start(groups[0])
        start(groups[1])
        for i in range(plan.steps):
            wait(groups[i])
            if i + 2 < plan.steps:
                start(groups[i + 2])
            elif i + 2 == plan.steps:
                start(features[-1])
            for step in range(i + 1):
                for t in range(min(i + 1, plan.blocks)):
                    if step == i or t == i:
                        down = plan.dots(step, t, w_ref, g_ref, cat, scaled)
                        if step == 0:
                            rows = slice(PROJ, 2 * PROJ)
                            if before_ref is not None:
                                down = down + before_ref[rows, plan.span(t)]
                            sums[rows, plan.span(t)] = down
        for t in range(plan.blocks):
            span = plan.span(t)
            up = jnp.dot(b_ref[...], scaled[:, span], preferred_element_type=F32)
            if before_ref is not None:
                up = up + before_ref[:PROJ, span]
            sums[:PROJ, span] = up
        wait(features[-1])
        total = plan.projections(proj)
        if before_ref is not None:
            total = total + before_ref[2 * PROJ :, :]
        sums[2 * PROJ :, :] = total

    operands = [core, chips, *pieces, in_hbm(weights), in_hbm(out_basis_t)]
    operands += [in_vmem(gates), basis_t]
    in_specs = [SMEM, SMEM] + [ANY] * (len(pieces) + 2) + [VMEM, VMEM]
    scratch = plan.scratch() + [pltpu.VMEM(plan.weights_shape, BF16), plan.weight_semaphores()]
    if before is not None:
        operands.append(before)
        in_specs.append(VMEM)
    return pl.pallas_call(
        body,
        in_specs=in_specs,
        out_specs=VMEM,
        out_shape=jax.ShapeDtypeStruct((3 * PROJ, tokens), F32),
        scratch_shapes=scratch,
        compiler_params=PARAMS,
        cost_estimate=plan.cost(),
        name="middle_stage",
    )(*operands)


def last_stage(
    core, chips, first_chip, lengths, pair_weights, pieces, before, weights, gates, basis_t, out_basis_t, act, seq_len, devices
):
    count = len(pieces) // NC
    height, tokens = pieces[0].shape
    hidden = gates.shape[0]
    plan = Stage(count, height - PROJ, hidden, tokens)
    pair_tokens = 2 * seq_len
    pairs = tokens // pair_tokens
    share = PROJ // devices

    def body(core_ref, chips_ref, lengths_ref, pair_ref, *refs):
        piece_refs, refs = refs[: len(pieces)], refs[len(pieces) :]
        before_ref, w_hbm, out_hbm, g_ref, b_ref, act_ref, o_ref = refs[:7]
        cat, proj, scaled, sem, left, sums, act_sem, w_ref, w_sem = refs[7:]
        columns = plan.weight_copies(chips_ref, first_chip, w_hbm, out_hbm, w_ref, w_sem)
        features = plan.feature_copies(core_ref[0], piece_refs, cat, proj, sem)
        act_copy = pltpu.make_async_copy(act_ref, left.at[pl.ds(PROJ, PROJ)], act_sem)
        start(features[0])
        for group in columns:
            start(group)
        start(features[1] + [act_copy])
        for t in range(plan.blocks):
            wait(features[t])
            if t + 2 <= plan.blocks:
                start(features[t + 2])
            span = plan.span(t)
            for step in range(plan.steps):
                if t == 0:
                    wait(columns[step])
                down = plan.dots(step, t, w_ref, g_ref, cat, scaled)
                if step == 0:
                    sums[PROJ:, span] = down + before_ref[PROJ : 2 * PROJ, span]
            up = jnp.dot(b_ref[...], scaled[:, span], preferred_element_type=F32)
            sums[:PROJ, span] = up + before_ref[:PROJ, span]
        wait(features[-1] + [act_copy])
        left[:PROJ, :] = plan.projections(proj) + before_ref[2 * PROJ :, :]
        lane = lax.broadcasted_iota(jnp.int32, (1, seq_len), 1)
        for s in range(tokens // seq_len):
            columns = slice(s * seq_len, (s + 1) * seq_len)
            sign = 1.0 if s % 2 == 0 else -1.0
            factor = jnp.where(lane < lengths_ref[s // 2, s % 2], pair_ref[s // 2] * sign, 0.0)
            left[:, columns] = left[:, columns] * factor
        half = lax.broadcasted_iota(jnp.int32, (PROJ, LANES), 1) < PROJ
        for pair in range(pairs):
            span = slice(pair * pair_tokens, (pair + 1) * pair_tokens)
            a, b = left[:, span], sums[:, span]
            a_high, b_high = a.astype(BF16), b.astype(BF16)
            a_low, b_low = (a - a_high.astype(F32)).astype(BF16), (b - b_high.astype(F32)).astype(BF16)
            both = dot_t(
                jnp.concatenate([a_high, a_high, a_low], axis=1), jnp.concatenate([b_high, b_low, b_high], axis=1)
            )
            grads = jnp.where(half, both[:PROJ], both[PROJ:])
            for c in range(NC):
                blocks = [grads[k * share : (k + 1) * share] for k in range(c, devices, NC)]
                mine = jnp.concatenate(blocks, axis=0).astype(BF16)
                for k in range(c, devices, NC):
                    o_ref[k, pair * PROJ // NC : (pair + 1) * PROJ // NC, :] = mine

    return pl.pallas_call(
        body,
        in_specs=[SMEM] * 4 + [ANY] * len(pieces) + [VMEM, ANY, ANY, VMEM, VMEM, ANY],
        out_specs=VMEM,
        out_shape=jax.ShapeDtypeStruct((devices, pairs * PROJ // NC, LANES), BF16),
        scratch_shapes=plan.scratch()
        + [pltpu.VMEM((2 * PROJ, tokens), F32), pltpu.VMEM((2 * PROJ, tokens), F32), pltpu.SemaphoreType.DMA]
        + [pltpu.VMEM(plan.weights_shape, BF16), plan.weight_semaphores()],
        compiler_params=PARAMS,
        cost_estimate=plan.cost(),
        name="last_stage",
    )(
        core, chips, lengths, pair_weights, *pieces,
        before, in_hbm(weights), in_hbm(out_basis_t), in_vmem(gates), basis_t, in_hbm(act),
    )


def shards(
    inputs,
    cotangent,
    gate_pre,
    up_out,
    w_down,
    up_in_basis,
    up_out_basis,
    down_in_basis,
    down_out_basis,
    lengths,
    margins,
    curvature,
):
    pair_count = inputs.shape[0]
    seq_len = inputs.shape[2]
    width = inputs.shape[3]
    hidden = gate_pre.shape[3]
    token_count = pair_count * 2 * seq_len
    train_count = pair_count - QUERY_DEV
    dp_size = lax.axis_size("dp")
    tensor_size = lax.axis_size("tensor")
    row_share = PROJ // tensor_size
    place = lax.axis_index("tensor")
    x, y, core = place // (NY * NC), (place // NC) % NY, place % NC

    own = first(
        place[None],
        cotangent.reshape(token_count, width),
        inputs.reshape(token_count, width),
        up_in_basis.T,
    )
    gates, act = prepare(
        gate_pre.reshape(token_count, hidden),
        up_out.reshape(token_count, hidden),
        down_in_basis.T,
    )
    pair_weights = 1.0 / (1.0 + jnp.exp(margins))

    def chip_at(dx, row):
        return ((x + dx) % NX) * NY + row

    flip = 1 - y
    near_chips = [chip_at(0, y), chip_at(3, y), chip_at(1, y), chip_at(0, flip)]
    opposite, bend = chip_at(2, y), chip_at(3, flip)
    far_chips = [jnp.where(core == 0, opposite, bend), chip_at(1, flip), jnp.where(core == 0, bend, opposite)]
    far_chips.append(chip_at(2, flip))
    chips = jnp.stack(near_chips + far_chips).astype(jnp.int32)
    bases = (up_out_basis.T, down_out_basis.T)

    def with_twins(pieces):
        return [shard for piece in pieces for shard in (piece, send(piece, CORE_SWAP))]

    near = (send(own, X_UP), send(own, X_DOWN), send(own, Y_SWAP))
    sums = middle_stage(core[None], chips, 0, with_twins([own]), w_down, gates, *bases)
    near = [lax.optimization_barrier((piece, sums))[0] for piece in near]
    left_own, right_own, across = near
    straight, right_across, bent = send(left_own, X_OR_Y), send(across, X_DOWN), send(left_own, Y_OR_X)
    sums = middle_stage(core[None], chips, 1, with_twins(near), w_down, gates, *bases, before=sums)
    far = [lax.optimization_barrier((piece, sums))[0] for piece in (straight, right_across, bent)]
    last_hop = send(far[0], Y_OR_X)
    twins = [send(piece, CORE_SWAP) for piece in far]
    shards = [far[0], twins[2], far[1], twins[1], far[2], twins[0]]
    sums = middle_stage(core[None], chips, 4, shards, w_down, gates, *bases, before=sums)
    last_hop, sums = lax.optimization_barrier((last_hop, sums))
    grads = last_stage(
        core[None], chips, 7, lengths, pair_weights, with_twins([last_hop]),
        sums, w_down, gates, *bases, act, seq_len, tensor_size,
    )
    grad_parts = lax.all_to_all(grads, "tensor", 0, 0, tiled=True)
    half_rows = PROJ // NC
    rows = jnp.sum(grad_parts.astype(F32), axis=0).reshape(pair_count, half_rows, LANES)
    train_rows, query_rows = rows[:train_count], rows[train_count:]
    query_all = lax.all_to_all(
        jnp.broadcast_to(query_rows.astype(BF16), (dp_size, half_rows, LANES)), "dp", 0, 0, tiled=True
    )

    own_curvature = lax.dynamic_index_in_dim(
        curvature.reshape(2, tensor_size // NC, NC, row_share, PROJ), core, 2, keepdims=False
    )
    own_curvature = own_curvature.transpose(1, 2, 0, 3).reshape(half_rows, LANES)
    weighted = own_curvature[None] * train_rows
    self_part = jnp.sum(weighted * train_rows, axis=(1, 2))
    cross_part = jnp.sum(query_all.astype(F32)[:, None] * weighted[None], axis=(2, 3))
    sums = jnp.concatenate([cross_part, self_part[None]], axis=0)
    sums = sums + send(sums, CORE_SWAP)
    scores = sums[:dp_size] / jnp.sqrt(sums[dp_size:] + epsilon)
    train_own = lax.dynamic_slice_in_dim(train_rows, place // NC * row_share, row_share, 1)
    train_block = train_own.reshape(train_count, row_share, 2, PROJ).transpose(0, 2, 1, 3)
    return train_block, scores


def solution(mesh):
    return jax.shard_map(
        shards,
        mesh=mesh,
        in_specs=(
            P("dp", None, None, "tensor"),
            P("dp", None, None, "tensor"),
            P("dp", None, None, "tensor"),
            P("dp", None, None, "tensor"),
            P("tensor", None),
            P(),
            P("tensor", None),
            P("tensor", None),
            P(),
            P("dp", None),
            P("dp"),
            P(),
        ),
        out_specs=(P("dp", None, "tensor", None), P(None, "dp")),
        check_vma=False,
    )
```
